32 devices in a mesh: outer: 8 (over z, core), inner: 4 (over y, x).
Axes of the slice: x: 2, y: 2, z: 4, core: 2. Of those that a mesh axis runs over, the one named last changes fastest.
Arguments:
- tokens: bfloat16 [4096, 12288], P(('outer', 'inner')), may hold values from -16 to 16
- cotangent: bfloat16 [4096, 128], P(('outer', 'inner')), may hold values from -8 to 8
- secondary: bfloat16 [12288, 128], P('inner'), may hold values from -0.0546875 to 0.0546875
- master: float32 [12288, 128], P(('inner', 'outer')), may hold values from -6 to 6
- m_code: bfloat16 [12288, 128], P(('inner', 'outer')), may hold values from -1 to 1
- v_code: bfloat16 [12288, 128], P(('inner', 'outer')), may hold values from 0.049804688 to 1
- m_scale: float32 [3072], P(('inner', 'outer')), may hold values from 0.02 to 0.2
- v_scale: float32 [3072], P(('inner', 'outer')), may hold values from 0.001 to 0.02
Outputs:
- projected: bfloat16 [4096, 128], P(('outer', 'inner'))
- master_new: float32 [12288, 128], P(('inner', 'outer'))
- m_code_new: bfloat16 [12288, 128], P(('inner', 'outer'))
- v_code_new: bfloat16 [12288, 128], P(('inner', 'outer'))
- m_scale_new: float32 [3072], P(('inner', 'outer'))
- v_scale_new: float32 [3072], P(('inner', 'outer'))
- secondary_new: bfloat16 [12288, 128], P('inner')
The draws below stay inside these ranges and needn't reach their ends.
All inputs are finite; a program needn't handle non-finite values. Where the reference program divides by a largest or mean magnitude, that divisor is 1e-20 or more.
Results may differ from the reference program's by a relative error of at most 0.009.
Values may be sent and summed in bfloat16 or wider, within the bound.
A program may use at most 64 MiB of HBM per device.

```python
import math
import jax
import jax.numpy as jnp
from jax import lax

D = 12288
HEAD = 128
TOK_DEV = 128
TOKENS = 4096
BLOCKS = 3072
N_OUTER = 8
N_INNER = 4


def shared_signs(key):
    drawn = jax.random.randint(jax.random.fold_in(key, 31), (TOKENS,), 0, 2)
    return drawn.astype(jnp.float32) * 2.0 - 1.0


def shared_weight():
    return 2.0 ** 0.5 / float(TOKENS) ** 0.25


def draw_tokens(key, part):
    devices = TOKENS // TOK_DEV
    shard_rows = D // devices
    column = jnp.arange(D, dtype=jnp.int32)
    owner = column // shard_rows
    outer_index = (owner % N_OUTER).astype(jnp.float32)
    variance = 0.5 + outer_index / max(N_OUTER - 1, 1)
    amplitude = jnp.sqrt(variance)
    base = jax.random.normal(jax.random.fold_in(key, 11), (TOKENS, D), jnp.float32)
    base = jnp.clip(base, -4.0, 4.0)
    pairing = jax.random.permutation(jax.random.fold_in(key, 12), devices).astype(jnp.int32)
    row_group = jnp.arange(TOKENS, dtype=jnp.int32) // TOK_DEV
    spiked = pairing[row_group][:, None] == owner[None, :]
    boost = jnp.where(spiked, 6.0, 1.0)
    direction = jnp.clip(jax.random.normal(jax.random.fold_in(key, 13), (D,), jnp.float32), -3.0, 3.0)
    signs = shared_signs(key)
    common = shared_weight() * signs[:, None] * direction[None, :]
    values = (base * boost + common) * amplitude[None, :]
    return jnp.clip(values, -16.0, 16.0).astype(jnp.bfloat16)


def draw_cotangent(key, part):
    base = jnp.clip(jax.random.normal(jax.random.fold_in(key, 41), (TOKENS, HEAD), jnp.float32), -4.0, 4.0)
    direction = jnp.clip(jax.random.normal(jax.random.fold_in(key, 42), (HEAD,), jnp.float32), -3.0, 3.0)
    signs = shared_signs(key)
    values = base + shared_weight() * signs[:, None] * direction[None, :]
    return jnp.clip(values, -8.0, 8.0).astype(jnp.bfloat16)


def levels(key, dims, split, low, high):
    factor_of, own = 1.0, jax.random.fold_in(key, 6)
    for position, shards_of in split:
        heights = jnp.exp(jax.random.uniform(jax.random.fold_in(own, position), (shards_of,), jnp.float32, low / len(split), high / len(split)))
        factor_of = factor_of * jnp.repeat(heights, dims[position] // shards_of).reshape([-1 if axis == position else 1 for axis in range(len(dims))])
    return factor_of


def gaussian(stream_key, extent, deviation, bound, pieces=(), held_as=jnp.bfloat16):
    loudness = levels(stream_key, extent, pieces, -0.22, 0.18) if pieces else 1.0
    array = jax.random.normal(stream_key, extent, jnp.float32) * deviation * loudness
    return jnp.minimum(jnp.maximum(array, -bound), bound).astype(held_as)


def setup_inputs(seed: int = 0) -> dict:
    splits = jax.random.split(jax.random.key(seed), 9)
    return {
        "tokens": draw_tokens(jax.random.fold_in(splits[8], 71), 0),
        "cotangent": draw_cotangent(jax.random.fold_in(splits[8], 71), 0),
        "secondary": gaussian(splits[2], (D, HEAD), D ** -0.5, 0.0546875, ((0, 4),)),
        "master": gaussian(splits[3], (D, HEAD), 1.0, 6.0, ((0, 32),), jnp.float32),
        "m_code": jnp.clip(jax.random.uniform(splits[4], (D, HEAD), jnp.float32, -1.0, 1.0) * levels(splits[4], (D, HEAD), ((0, 32),), -0.4, 0.0), -1.0, 1.0).astype(jnp.bfloat16),
        "v_code": jnp.clip(0.049804688 + 0.9501953 * jax.random.uniform(splits[5], (D, HEAD), jnp.float32) ** levels(splits[5], (D, HEAD), ((0, 32),), -0.2, 0.2), 0.049804688, 1.0).astype(jnp.bfloat16),
        "m_scale": jnp.clip(jnp.exp(math.log(0.2) - 2.3025851 * jax.random.uniform(splits[6], (BLOCKS,), jnp.float32) ** levels(splits[6], (BLOCKS,), ((0, 32),), -0.2, 0.2)), 0.02, 0.2),
        "v_scale": jnp.clip(jnp.exp(math.log(0.02) - 2.9957322 * jax.random.uniform(splits[7], (BLOCKS,), jnp.float32) ** levels(splits[7], (BLOCKS,), ((0, 32),), -0.2, 0.2)), 0.001, 0.02),
    }


def adam_update(gradient, factor, master, m_code, v_code, m_scale, v_scale):
    blocks = m_scale.shape[0]
    height = master.shape[0] // blocks
    shaped = (blocks, height, master.shape[1])
    m_old = (m_code.astype(jnp.float32).reshape(shaped) * m_scale[:, None, None]).reshape(master.shape)
    v_old = (v_code.astype(jnp.float32).reshape(shaped) * v_scale[:, None, None]).reshape(master.shape)
    scaled = factor * gradient
    moment = 0.9 * m_old + 0.1 * scaled
    second = 0.95 * v_old + 0.05 * scaled * scaled
    master_new = master - 0.01 * (moment / (jnp.sqrt(second) + 1e-08) + 0.1 * master)
    moment_blocks = moment.reshape(blocks, -1)
    second_blocks = second.reshape(blocks, -1)
    m_scale_new = lax.optimization_barrier(jnp.max(jnp.abs(moment_blocks), axis=1)) + 1e-06
    v_scale_new = lax.optimization_barrier(jnp.max(second_blocks, axis=1)) + 1e-06
    m_code_new = (moment_blocks / m_scale_new[:, None]).reshape(master.shape).astype(jnp.bfloat16)
    v_code_new = (second_blocks / v_scale_new[:, None]).reshape(master.shape).astype(jnp.bfloat16)
    return (master_new, m_code_new, v_code_new, m_scale_new, v_scale_new)

def reference(tokens, cotangent, secondary, master, m_code, v_code, m_scale, v_scale):
    projected = jnp.dot(tokens, secondary, preferred_element_type=jnp.float32).astype(jnp.bfloat16)
    groups = N_OUTER * N_INNER
    tok_blocks = tokens.reshape(groups, TOK_DEV, D)
    cot_blocks = cotangent.reshape(groups, TOK_DEV, HEAD)

    def accumulate(total, pair):
        part = lax.dot_general(pair[0], pair[1], (((0,), (0,)), ((), ())), preferred_element_type=jnp.float32)
        part = lax.optimization_barrier(part.astype(jnp.bfloat16))
        return (total + part.astype(jnp.float32), None)
    gradient, _ = lax.scan(accumulate, jnp.zeros((D, HEAD), jnp.float32), (tok_blocks, cot_blocks))
    total = jnp.sum(gradient * gradient)
    limit = 0.25 * math.sqrt(D * HEAD)
    factor = limit / jnp.maximum(jnp.sqrt(total), limit)
    master_new, m_code_new, v_code_new, m_scale_new, v_scale_new = adam_update(gradient, factor, master, m_code, v_code, m_scale, v_scale)
    secondary_new = master_new.astype(jnp.bfloat16)
    return (projected, master_new, m_code_new, v_code_new, m_scale_new, v_scale_new, secondary_new)
```

```python
import functools
import math

import jax
import jax.numpy as jnp
from jax import lax
from jax.experimental import pallas as pl
from jax.experimental.pallas import tpu as pltpu
from jax.sharding import PartitionSpec as P

MESH = pl.DeviceIdType.MESH
PIECE = 128
STEPS = (2, 1, 3, 0)


def adam_update(gradient, factor, master, m_code, v_code, m_scale, v_scale):
    blocks = m_scale.shape[0]
    height = master.shape[0] // blocks
    shaped = (blocks, height, master.shape[1])
    m_old = (m_code.astype(jnp.float32).reshape(shaped) * m_scale[:, None, None]).reshape(
        master.shape
    )
    v_old = (v_code.astype(jnp.float32).reshape(shaped) * v_scale[:, None, None]).reshape(
        master.shape
    )
    scaled = factor * gradient
    moment = 0.9 * m_old + 0.1 * scaled
    second = 0.95 * v_old + 0.05 * scaled * scaled
    master_new = master - 0.01 * (moment / (jnp.sqrt(second) + 1e-08) + 0.1 * master)
    moment_blocks = moment.reshape(blocks, -1)
    second_blocks = second.reshape(blocks, -1)
    m_scale_new = jnp.max(jnp.abs(moment_blocks), axis=1) + 1e-06
    v_scale_new = jnp.max(second_blocks, axis=1) + 1e-06
    m_code_new = (moment_blocks / m_scale_new[:, None]).reshape(master.shape).astype(jnp.bfloat16)
    v_code_new = (second_blocks / v_scale_new[:, None]).reshape(master.shape).astype(jnp.bfloat16)
    return (master_new, m_code_new, v_code_new, m_scale_new, v_scale_new)


def rounded_term(columns, cotangent):
    part = lax.dot_general(
        columns, cotangent, (((0,), (0,)), ((), ())), preferred_element_type=jnp.float32
    )
    part = lax.optimization_barrier(part.astype(jnp.bfloat16))
    return part.astype(jnp.float32)


def body(tokens, cotangent, secondary, master, m_code, v_code, m_scale, v_scale):
    tok_rows = tokens.shape[0]
    width = tokens.shape[1]
    n_outer = lax.axis_size("outer")
    n_inner = lax.axis_size("inner")
    columns = tokens
    projected = jnp.dot(
        columns,
        lax.all_gather(secondary, "inner", axis=0, tiled=True),
        preferred_element_type=jnp.float32,
    ).astype(jnp.bfloat16)
    reordered = (
        tokens.reshape(tok_rows, n_inner, n_outer, -1)
        .transpose(0, 2, 1, 3)
        .reshape(tok_rows, width)
    )
    columns = reordered
    gradient = lax.psum_scatter(
        rounded_term(columns, cotangent), ("outer", "inner"), scatter_dimension=0, tiled=True
    )
    total = lax.psum(jnp.sum(gradient * gradient), ("outer", "inner"))
    limit = 0.25 * math.sqrt(width * secondary.shape[1])
    factor = limit / jnp.maximum(jnp.sqrt(total), limit)
    master_new, m_code_new, v_code_new, m_scale_new, v_scale_new = adam_update(
        gradient, factor, master, m_code, v_code, m_scale, v_scale
    )
    secondary_new = lax.all_gather(master_new.astype(jnp.bfloat16), "outer", axis=0, tiled=True)
    return (projected, master_new, m_code_new, v_code_new, m_scale_new, v_scale_new, secondary_new)


def step_kernel(
    limit,
    tok, cot, sec, master, m_code, v_code, m_scale, v_scale,
    projected, master_new, m_code_new, v_code_new, m_scale_new, v_scale_new, sec_new,
    send_a, recv_a, send_1, recv_1, sum_2, send_2, recv_2, sum_3, send_3, recv_3,
    weights, sq_1, sq_2, sq_send, moments, seconds,
    sem_a, sem_1, sem_2, sem_3, sem_w, sem_f, sem_q1, sem_q2, sem_g, sem_h,
):
    f32, bf16 = jnp.float32, jnp.bfloat16
    o, i = lax.axis_index("outer"), lax.axis_index("inner")
    n_z = 4
    core, z = o % 2, o // 2
    x, y = i % 2, i // 2
    to_x, to_y = i + 1 - 2 * x, i + 2 - 4 * y
    first = to_x * (1 - core) + to_y * core
    second = to_x * core + to_y * (1 - core)
    across = 3 - i
    mate = o + 1 - 2 * core
    rows = master.shape[0]
    half = sec.shape[0] // 2
    span = sec.shape[0]

    barrier = pltpu.get_barrier_semaphore()
    near = [(o, first), (o, second), (o, across)]
    far = [((o + d) % 8, i) for d in range(1, 8)]
    for peer in near + far:
        pl.semaphore_signal(barrier, inc=1, device_id=peer, device_id_type=MESH)

    started = []

    def send(src, dst, sems, index, peer):
        copy = pltpu.make_async_remote_copy(
            src_ref=src, dst_ref=dst,
            send_sem=sems.at[0, index], recv_sem=sems.at[1, index],
            device_id=peer, device_id_type=MESH,
        )
        copy.start()
        started.append(copy)
        return copy

    def arrived(dst, sems, index):
        pltpu.make_async_remote_copy(
            src_ref=dst, dst_ref=dst,
            send_sem=sems.at[0, index], recv_sem=sems.at[1, index],
            device_id=(mate, i), device_id_type=MESH,
        ).wait_recv()

    def partial(j, s, c):
        block = j * 8 + ((z + STEPS[s]) % n_z) * 2 + c
        columns = tok[:, pl.ds(pl.multiple_of(block * rows, 128), rows)]
        return lax.dot_general(
            columns, cot[...], (((0,), (0,)), ((), ())), preferred_element_type=f32
        )

    for q, j in enumerate((across, second, first, i)):
        for s in range(4):
            send_a[q, s] = partial(j, s, 1 - core).astype(bf16)
            if q == 0 and s == 0:
                pl.semaphore_wait(barrier, 10)
            send(send_a.at[q, s], recv_a.at[q, s], sem_a, q * 4 + s, (mate, i))

    def chip_sum(q, j, s):
        own = partial(j, s, core)
        arrived(recv_a.at[q, s], sem_a, q * 4 + s)
        return own + recv_a[q, s].astype(f32)

    for q, j in enumerate((across, first)):
        for s in range(4):
            send_1[q, s] = chip_sum(q, j, s).astype(bf16)
            send(send_1.at[q, s], recv_1.at[q, s], sem_1, q * 4 + s, (o, first))
    for s in range(4):
        sum_2[s] = chip_sum(2, second, s)
    for s in range(4):
        arrived(recv_1.at[0, s], sem_1, s)
        send_2[s] = (sum_2[s] + recv_1[0, s].astype(f32)).astype(bf16)
        send(send_2.at[s], recv_2.at[s], sem_2, s, (o, second))
    for s in range(4):
        sum_3[s] = chip_sum(3, i, s)

    own_half = sec.at[pl.ds(pl.multiple_of(core * half, 128), half)]
    for index, peer in enumerate((first, second)):
        send(own_half, weights.at[i, core], sem_w, index, (o, peer))

    gradient = None
    for s in range(4):
        arrived(recv_1.at[1, s], sem_1, 4 + s)
        arrived(recv_2.at[s], sem_2, s)
        total = sum_3[s] + recv_1[1, s].astype(f32) + recv_2[s].astype(f32)
        if STEPS[s]:
            d = STEPS[s]
            send_3[d - 1] = total.astype(bf16)
            peer = ((z + d) % n_z) * 2 + core
            send(send_3.at[d - 1], recv_3.at[d - 1], sem_3, d - 1, (peer, i))
        else:
            sum_3[0] = total

    own_columns = tok[:, pl.ds(pl.multiple_of(i * span, 128), span)]
    out = jnp.dot(own_columns, sec[...], preferred_element_type=f32)

    for d in (1, 3, 2):
        arrived(recv_3.at[d - 1], sem_3, d - 1)
    gradient = sum_3[0]
    for d in range(1, 4):
        gradient = gradient + recv_3[d - 1].astype(f32)
    sum_3[0] = gradient

    squares = jnp.sum((gradient * gradient).reshape(rows // 8, 8, 128), axis=0)
    sq_send[0] = squares
    for index, peer in enumerate((first, second, across)):
        send(sq_send.at[0], sq_1.at[index], sem_q1, index, (o, peer))
    for index in range(3):
        arrived(sq_1.at[index], sem_q1, index)
        squares = squares + sq_1[index]
    sq_send[1] = squares
    for d in range(1, 8):
        send(sq_send.at[1], sq_2.at[d - 1], sem_q2, d - 1, ((o + d) % 8, i))

    height = rows // m_scale.shape[1]

    def block_mask(p):
        shape = (PIECE, m_scale.shape[1])
        row = lax.broadcasted_iota(jnp.int32, shape, 0) + p * PIECE
        return row // height == lax.broadcasted_iota(jnp.int32, shape, 1)

    def expand(p, scales):
        return jnp.sum(jnp.where(block_mask(p), scales, 0.0), axis=1, keepdims=True)

    pieces = rows // PIECE
    for p in range(pieces):
        part = pl.ds(p * PIECE, PIECE)
        moments[part, :] = 0.9 * (m_code[part, :].astype(f32) * expand(p, m_scale[...]))
        seconds[part, :] = 0.95 * (v_code[part, :].astype(f32) * expand(p, v_scale[...]))

    for d in range(1, 8):
        arrived(sq_2.at[d - 1], sem_q2, d - 1)
        squares = squares + sq_2[d - 1]
    square_sum = jnp.sum(jnp.sum(squares, axis=0, keepdims=True), axis=1, keepdims=True)
    factor = limit / jnp.maximum(jnp.sqrt(square_sum), limit)

    for p in range(pieces):
        part = pl.ds(p * PIECE, PIECE)
        scaled = factor * sum_3[0, part, :]
        moment = moments[part, :] + 0.1 * scaled
        second_new = seconds[part, :] + 0.05 * scaled * scaled
        old = master[part, :]
        new = old - 0.01 * (moment / (jnp.sqrt(second_new) + 1e-08) + 0.1 * old)
        moments[part, :] = moment
        seconds[part, :] = second_new
        master_new[part, :] = new
        sec_new[pl.ds(pl.multiple_of(o * rows + p * PIECE, 128), PIECE), :] = new.astype(bf16)

    def new_rows(owner):
        return sec_new.at[pl.ds(pl.multiple_of(owner * rows, 128), rows)]

    for d in (2, 1, 3):
        send(new_rows(o), new_rows(o), sem_g, d - 1, (((z + d) % n_z) * 2 + core, i))
    send(new_rows(o), new_rows(o), sem_h, 0, (mate, i))

    arrived(weights.at[first, core], sem_w, 0)
    send(weights.at[first, core], weights.at[first, core], sem_w, 2, (o, second))
    send(weights.at[first, core], weights.at[first, core], sem_f, 0, (mate, i))
    arrived(weights.at[second, core], sem_w, 1)
    send(weights.at[second, core], weights.at[second, core], sem_f, 1, (mate, i))

    m_row = jnp.zeros(m_scale.shape, f32)
    v_row = jnp.zeros(v_scale.shape, f32)
    for p in range(pieces):
        part = pl.ds(p * PIECE, PIECE)
        mask = block_mask(p)
        for values, codes, is_m in ((moments, m_code_new, True), (seconds, v_code_new, False)):
            value = values[part, :]
            tops = jnp.max(jnp.abs(value), axis=1, keepdims=True)
            top = jnp.max(jnp.where(mask, tops, 0.0), axis=0, keepdims=True)
            scale = top + 1e-06
            codes[part, :] = (value / expand(p, scale)).astype(bf16)
            if is_m:
                m_row = jnp.maximum(m_row, top)
            else:
                v_row = jnp.maximum(v_row, top)
    m_scale_new[...] = m_row + 1e-06
    v_scale_new[...] = v_row + 1e-06

    def product(j, h):
        start = pl.multiple_of(j * span + h * half, 128)
        return jnp.dot(tok[:, pl.ds(start, half)], weights[j, h], preferred_element_type=f32)

    out = out + product(first, core)
    out = out + product(second, core)

    def gathered(d):
        owner = ((z + n_z - d) % n_z) * 2 + core
        arrived(new_rows(owner), sem_g, d - 1)
        send(new_rows(owner), new_rows(owner), sem_h, d, (mate, i))

    gathered(1)
    arrived(weights.at[across, core], sem_w, 2)
    send(weights.at[across, core], weights.at[across, core], sem_f, 2, (mate, i))
    out = out + product(across, core)
    for index, j in enumerate((second, first)):
        arrived(weights.at[j, 1 - core], sem_f, index)
        out = out + product(j, 1 - core)
    gathered(3)
    arrived(weights.at[across, 1 - core], sem_f, 2)
    out = out + product(across, 1 - core)
    projected[...] = out.astype(bf16)
    gathered(2)
    for d in range(4):
        owner = ((z + n_z - d) % n_z) * 2 + 1 - core
        arrived(new_rows(owner), sem_h, d)
    for copy in started:
        copy.wait_send()


def fused_body(tokens, cotangent, secondary, master, m_code, v_code, m_scale, v_scale):
    f32, bf16 = jnp.float32, jnp.bfloat16
    rows, head = master.shape
    blocks = m_scale.shape[0]
    chunk = (rows, head)
    limit = 0.25 * math.sqrt(tokens.shape[1] * secondary.shape[1])
    vmem, dma = pltpu.VMEM, pltpu.SemaphoreType.DMA
    shapes = (
        ((tokens.shape[0], head), bf16),
        (chunk, f32),
        (chunk, bf16),
        (chunk, bf16),
        ((1, blocks), f32),
        ((1, blocks), f32),
        (secondary.shape, bf16),
    )
    work = 4 * tokens.shape[0] * tokens.shape[1] * head
    outs = pl.pallas_call(
        functools.partial(step_kernel, limit),
        out_shape=[jax.ShapeDtypeStruct(shape, dtype) for shape, dtype in shapes],
        in_specs=[pl.BlockSpec(memory_space=vmem)] * 8,
        out_specs=[pl.BlockSpec(memory_space=vmem)] * 7,
        scratch_shapes=[
            vmem((4, 4) + chunk, bf16),
            vmem((4, 4) + chunk, bf16),
            vmem((2, 4) + chunk, bf16),
            vmem((2, 4) + chunk, bf16),
            vmem((4,) + chunk, f32),
            vmem((4,) + chunk, bf16),
            vmem((4,) + chunk, bf16),
            vmem((4,) + chunk, f32),
            vmem((3,) + chunk, bf16),
            vmem((3,) + chunk, bf16),
            vmem((4, 2, secondary.shape[0] // 2, head), bf16),
            vmem((3, 8, head), f32),
            vmem((7, 8, head), f32),
            vmem((2, 8, head), f32),
            vmem(chunk, f32),
            vmem(chunk, f32),
            dma((2, 16)),
            dma((2, 8)),
            dma((2, 4)),
            dma((2, 3)),
            dma((2, 3)),
            dma((2, 3)),
            dma((2, 3)),
            dma((2, 7)),
            dma((2, 3)),
            dma((2, 4)),
        ],
        compiler_params=pltpu.CompilerParams(
            collective_id=0, has_side_effects=True, vmem_limit_bytes=48 * 1024 * 1024
        ),
        cost_estimate=pl.CostEstimate(flops=work, bytes_accessed=8 << 20, transcendentals=0),
    )(
        tokens, cotangent, secondary, master, m_code, v_code,
        m_scale.reshape(1, blocks), v_scale.reshape(1, blocks),
    )
    return (*outs[:4], outs[4].reshape(blocks), outs[5].reshape(blocks), outs[6])


def fits(mesh):
    return mesh.shape["outer"] == 8 and mesh.shape["inner"] == 4


def solution(mesh):
    in_specs = (
        P(("outer", "inner"), None),
        P(("outer", "inner"), None),
        P("inner", None),
        P(("inner", "outer"), None),
        P(("inner", "outer"), None),
        P(("inner", "outer"), None),
        P(("inner", "outer")),
        P(("inner", "outer")),
    )
    out_specs = (
        P(("outer", "inner"), None),
        P(("inner", "outer"), None),
        P(("inner", "outer"), None),
        P(("inner", "outer"), None),
        P(("inner", "outer")),
        P(("inner", "outer")),
        P("inner", None),
    )
    program = fused_body if fits(mesh) else body
    return jax.shard_map(
        program, mesh=mesh, in_specs=in_specs, out_specs=out_specs, check_vma=False
    )
```

```python
import functools
import math

import jax
import jax.numpy as jnp
from jax import lax
from jax.experimental import pallas as pl
from jax.experimental.pallas import tpu as pltpu
from jax.sharding import PartitionSpec as P

MESH = pl.DeviceIdType.MESH
PIECE = 128
VMEM_BYTES = 60 * 1024 * 1024
STEPS = (2, 1, 3, 0)


def adam_update(gradient, factor, master, m_code, v_code, m_scale, v_scale):
    blocks = m_scale.shape[0]
    height = master.shape[0] // blocks
    shaped = (blocks, height, master.shape[1])
    m_old = (m_code.astype(jnp.float32).reshape(shaped) * m_scale[:, None, None]).reshape(
        master.shape
    )
    v_old = (v_code.astype(jnp.float32).reshape(shaped) * v_scale[:, None, None]).reshape(
        master.shape
    )
    scaled = factor * gradient
    moment = 0.9 * m_old + 0.1 * scaled
    second = 0.95 * v_old + 0.05 * scaled * scaled
    master_new = master - 0.01 * (moment / (jnp.sqrt(second) + 1e-08) + 0.1 * master)
    moment_blocks = moment.reshape(blocks, -1)
    second_blocks = second.reshape(blocks, -1)
    m_scale_new = jnp.max(jnp.abs(moment_blocks), axis=1) + 1e-06
    v_scale_new = jnp.max(second_blocks, axis=1) + 1e-06
    m_code_new = (moment_blocks / m_scale_new[:, None]).reshape(master.shape).astype(jnp.bfloat16)
    v_code_new = (second_blocks / v_scale_new[:, None]).reshape(master.shape).astype(jnp.bfloat16)
    return (master_new, m_code_new, v_code_new, m_scale_new, v_scale_new)


def rounded_term(columns, cotangent):
    part = lax.dot_general(
        columns, cotangent, (((0,), (0,)), ((), ())), preferred_element_type=jnp.float32
    )
    part = lax.optimization_barrier(part.astype(jnp.bfloat16))
    return part.astype(jnp.float32)


def body(tokens, cotangent, secondary, master, m_code, v_code, m_scale, v_scale):
    tok_rows = tokens.shape[0]
    width = tokens.shape[1]
    n_outer = lax.axis_size("outer")
    n_inner = lax.axis_size("inner")
    columns = tokens
    projected = jnp.dot(
        columns,
        lax.all_gather(secondary, "inner", axis=0, tiled=True),
        preferred_element_type=jnp.float32,
    ).astype(jnp.bfloat16)
    reordered = (
        tokens.reshape(tok_rows, n_inner, n_outer, -1)
        .transpose(0, 2, 1, 3)
        .reshape(tok_rows, width)
    )
    columns = reordered
    gradient = lax.psum_scatter(
        rounded_term(columns, cotangent), ("outer", "inner"), scatter_dimension=0, tiled=True
    )
    total = lax.psum(jnp.sum(gradient * gradient), ("outer", "inner"))
    limit = 0.25 * math.sqrt(width * secondary.shape[1])
    factor = limit / jnp.maximum(jnp.sqrt(total), limit)
    master_new, m_code_new, v_code_new, m_scale_new, v_scale_new = adam_update(
        gradient, factor, master, m_code, v_code, m_scale, v_scale
    )
    secondary_new = lax.all_gather(master_new.astype(jnp.bfloat16), "outer", axis=0, tiled=True)
    return (projected, master_new, m_code_new, v_code_new, m_scale_new, v_scale_new, secondary_new)


def step_kernel(
    limit,
    tok_in, cot_in, sec_in, master_in, m_code_in, v_code_in, m_scale_in, v_scale_in,
    projected_out, master_out, m_code_out, v_code_out, m_scale_out, v_scale_out, sec_out,
    projected, master_new, m_code_new, v_code_new, m_scale_new, v_scale_new, sec_new,
    tok, cot, sec, master, m_code, v_code, m_scale, v_scale,
    send_a, recv_a, send_1, recv_1, sum_2, send_2, recv_2, sum_3, send_3, recv_3,
    weights, sq_1, sq_2, sq_send, moments, seconds,
    sem_in, sem_out, sem_a, sem_1, sem_2, sem_3, sem_w, sem_f, sem_q1, sem_q2, sem_g, sem_h,
):
    f32, bf16 = jnp.float32, jnp.bfloat16
    o, i = lax.axis_index("outer"), lax.axis_index("inner")
    n_z = 4
    core, z = o % 2, o // 2
    x, y = i % 2, i // 2
    to_x, to_y = i + 1 - 2 * x, i + 2 - 4 * y
    first = to_x * (1 - core) + to_y * core
    second = to_x * core + to_y * (1 - core)
    across = 3 - i
    mate = o + 1 - 2 * core
    rows = master.shape[0]
    half = sec.shape[0] // 2
    span = sec.shape[0]

    barrier = pltpu.get_barrier_semaphore()
    near = [(o, first), (o, second), (o, across)]
    far = [((o + d) % 8, i) for d in range(1, 8)]
    for peer in near + far:
        pl.semaphore_signal(barrier, inc=1, device_id=peer, device_id_type=MESH)

    loads = []

    def load(src, dst):
        loads.append(pltpu.make_async_copy(src, dst, sem_in.at[len(loads)]))
        loads[-1].start()

    stores = []

    def store(src, dst):
        stores.append(pltpu.make_async_copy(src, dst, sem_out.at[len(stores)]))
        stores[-1].start()

    load(cot_in, cot)
    for j in (across, second, first, i):
        columns = pl.ds(pl.multiple_of(j * span, 128), span)
        load(tok_in.at[:, columns], tok.at[:, columns])
    load(sec_in, sec)
    load(master_in, master)
    load(m_code_in, m_code)
    load(v_code_in, v_code)
    load(m_scale_in, m_scale)
    load(v_scale_in, v_scale)

    started = []

    def send(src, dst, sems, index, peer):
        copy = pltpu.make_async_remote_copy(
            src_ref=src, dst_ref=dst,
            send_sem=sems.at[0, index], recv_sem=sems.at[1, index],
            device_id=peer, device_id_type=MESH,
        )
        copy.start()
        started.append(copy)
        return copy

    def arrived(dst, sems, index):
        pltpu.make_async_remote_copy(
            src_ref=dst, dst_ref=dst,
            send_sem=sems.at[0, index], recv_sem=sems.at[1, index],
            device_id=(mate, i), device_id_type=MESH,
        ).wait_recv()

    def partial(j, s, c):
        block = j * 8 + ((z + STEPS[s]) % n_z) * 2 + c
        columns = tok[:, pl.ds(pl.multiple_of(block * rows, 128), rows)]
        return lax.dot_general(
            columns, cot[...], (((0,), (0,)), ((), ())), preferred_element_type=f32
        )

    mate_groups = (across, second, first, i)
    own_groups = (across, first, second, i)

    def for_mate(q):
        for s in range(4):
            send_a[q, s] = partial(mate_groups[q], s, 1 - core).astype(bf16)
            if q == 0 and s == 0:
                pl.semaphore_wait(barrier, 10)
            send(send_a.at[q, s], recv_a.at[q, s], sem_a, q * 4 + s, (mate, i))

    def chip_sum(q, s):
        own = partial(own_groups[q], s, core)
        arrived(recv_a.at[q, s], sem_a, q * 4 + s)
        return own + recv_a[q, s].astype(f32)

    def to_first(q):
        for s in range(4):
            send_1[q, s] = chip_sum(q, s).astype(bf16)
            send(send_1.at[q, s], recv_1.at[q, s], sem_1, q * 4 + s, (o, first))

    loads[0].wait()
    loads[1].wait()
    for_mate(0)
    loads[2].wait()
    for_mate(1)
    to_first(0)
    loads[3].wait()
    for_mate(2)
    to_first(1)
    loads[4].wait()
    for_mate(3)
    for s in range(4):
        sum_2[s] = chip_sum(2, s)
    for s in range(4):
        sum_3[s] = chip_sum(3, s)
    for s in range(4):
        arrived(recv_1.at[0, s], sem_1, s)
        send_2[s] = (sum_2[s] + recv_1[0, s].astype(f32)).astype(bf16)
        send(send_2.at[s], recv_2.at[s], sem_2, s, (o, second))

    for s in range(4):
        arrived(recv_1.at[1, s], sem_1, 4 + s)
        arrived(recv_2.at[s], sem_2, s)
        total = sum_3[s] + recv_1[1, s].astype(f32) + recv_2[s].astype(f32)
        if STEPS[s]:
            d = STEPS[s]
            send_3[d - 1] = total.astype(bf16)
            peer = ((z + d) % n_z) * 2 + core
            send(send_3.at[d - 1], recv_3.at[d - 1], sem_3, d - 1, (peer, i))
        else:
            sum_3[0] = total

    loads[5].wait()
    own_half = sec.at[pl.ds(pl.multiple_of(core * half, 128), half)]
    for index, peer in enumerate((first, second)):
        send(own_half, weights.at[i, core], sem_w, index, (o, peer))

    own_columns = tok[:, pl.ds(pl.multiple_of(i * span, 128), span)]
    out = jnp.dot(own_columns, sec[...], preferred_element_type=f32)

    for d in (1, 3, 2):
        arrived(recv_3.at[d - 1], sem_3, d - 1)
    gradient = sum_3[0]
    for d in range(1, 4):
        gradient = gradient + recv_3[d - 1].astype(f32)
    sum_3[0] = gradient

    squares = jnp.sum((gradient * gradient).reshape(rows // 8, 8, 128), axis=0)
    sq_send[0] = squares
    for index, peer in enumerate((first, second, across)):
        send(sq_send.at[0], sq_1.at[index], sem_q1, index, (o, peer))
    for index in range(3):
        arrived(sq_1.at[index], sem_q1, index)
        squares = squares + sq_1[index]
    sq_send[1] = squares
    for d in range(1, 8):
        send(sq_send.at[1], sq_2.at[d - 1], sem_q2, d - 1, ((o + d) % 8, i))

    for copy in loads[6:]:
        copy.wait()
    height = rows // m_scale.shape[1]

    def block_mask(p):
        shape = (PIECE, m_scale.shape[1])
        row = lax.broadcasted_iota(jnp.int32, shape, 0) + p * PIECE
        return row // height == lax.broadcasted_iota(jnp.int32, shape, 1)

    def expand(p, scales):
        return jnp.sum(jnp.where(block_mask(p), scales, 0.0), axis=1, keepdims=True)

    pieces = rows // PIECE
    for p in range(pieces):
        part = pl.ds(p * PIECE, PIECE)
        moments[part, :] = 0.9 * (m_code[part, :].astype(f32) * expand(p, m_scale[...]))
        seconds[part, :] = 0.95 * (v_code[part, :].astype(f32) * expand(p, v_scale[...]))

    for d in range(1, 8):
        arrived(sq_2.at[d - 1], sem_q2, d - 1)
        squares = squares + sq_2[d - 1]
    square_sum = jnp.sum(jnp.sum(squares, axis=0, keepdims=True), axis=1, keepdims=True)
    factor = limit / jnp.maximum(jnp.sqrt(square_sum), limit)

    for p in range(pieces):
        part = pl.ds(p * PIECE, PIECE)
        scaled = factor * sum_3[0, part, :]
        moment = moments[part, :] + 0.1 * scaled
        second_new = seconds[part, :] + 0.05 * scaled * scaled
        old = master[part, :]
        new = old - 0.01 * (moment / (jnp.sqrt(second_new) + 1e-08) + 0.1 * old)
        moments[part, :] = moment
        seconds[part, :] = second_new
        master_new[part, :] = new
        sec_new[pl.ds(pl.multiple_of(o * rows + p * PIECE, 128), PIECE), :] = new.astype(bf16)

    def new_rows(owner):
        return sec_new.at[pl.ds(pl.multiple_of(owner * rows, 128), rows)]

    def store_rows(owner):
        store(new_rows(owner), sec_out.at[pl.ds(pl.multiple_of(owner * rows, 128), rows)])

    for d in (2, 1, 3):
        send(new_rows(o), new_rows(o), sem_g, d - 1, (((z + d) % n_z) * 2 + core, i))
    send(new_rows(o), new_rows(o), sem_h, 0, (mate, i))
    store(master_new, master_out)
    store_rows(o)

    arrived(weights.at[first, core], sem_w, 0)
    send(weights.at[first, core], weights.at[first, core], sem_w, 2, (o, second))
    send(weights.at[first, core], weights.at[first, core], sem_f, 0, (mate, i))
    arrived(weights.at[second, core], sem_w, 1)
    send(weights.at[second, core], weights.at[second, core], sem_f, 1, (mate, i))

    m_row = jnp.zeros(m_scale.shape, f32)
    v_row = jnp.zeros(v_scale.shape, f32)
    for p in range(pieces):
        part = pl.ds(p * PIECE, PIECE)
        mask = block_mask(p)
        for values, codes, is_m in ((moments, m_code_new, True), (seconds, v_code_new, False)):
            value = values[part, :]
            tops = jnp.max(jnp.abs(value), axis=1, keepdims=True)
            top = jnp.max(jnp.where(mask, tops, 0.0), axis=0, keepdims=True)
            scale = top + 1e-06
            codes[part, :] = (value / expand(p, scale)).astype(bf16)
            if is_m:
                m_row = jnp.maximum(m_row, top)
            else:
                v_row = jnp.maximum(v_row, top)
    m_scale_new[...] = m_row + 1e-06
    v_scale_new[...] = v_row + 1e-06
    store(m_code_new, m_code_out)
    store(v_code_new, v_code_out)
    store(m_scale_new, m_scale_out)
    store(v_scale_new, v_scale_out)

    def product(j, h):
        start = pl.multiple_of(j * span + h * half, 128)
        return jnp.dot(tok[:, pl.ds(start, half)], weights[j, h], preferred_element_type=f32)

    out = out + product(first, core)
    out = out + product(second, core)

    def gathered(d):
        owner = ((z + n_z - d) % n_z) * 2 + core
        arrived(new_rows(owner), sem_g, d - 1)
        send(new_rows(owner), new_rows(owner), sem_h, d, (mate, i))
        store_rows(owner)

    gathered(1)
    arrived(weights.at[across, core], sem_w, 2)
    send(weights.at[across, core], weights.at[across, core], sem_f, 2, (mate, i))
    out = out + product(across, core)
    for index, j in enumerate((second, first)):
        arrived(weights.at[j, 1 - core], sem_f, index)
        out = out + product(j, 1 - core)
    gathered(3)
    arrived(weights.at[across, 1 - core], sem_f, 2)
    out = out + product(across, 1 - core)
    projected[...] = out.astype(bf16)
    store(projected, projected_out)
    gathered(2)
    for d in range(4):
        owner = ((z + n_z - d) % n_z) * 2 + 1 - core
        arrived(new_rows(owner), sem_h, d)
        store_rows(owner)
    for copy in stores:
        copy.wait()
    for copy in started:
        copy.wait_send()


def write_kernel(*refs):
    count = len(refs) // 2
    sems = refs[-1]
    copies = [
        pltpu.make_async_copy(refs[k], refs[count + k], sems.at[k]) for k in range(count)
    ]
    for copy in copies:
        copy.start()
    for copy in copies:
        copy.wait()


def fused_body(tokens, cotangent, secondary, master, m_code, v_code, m_scale, v_scale):
    f32, bf16 = jnp.float32, jnp.bfloat16
    rows, head = master.shape
    blocks = m_scale.shape[0]
    chunk = (rows, head)
    limit = 0.25 * math.sqrt(tokens.shape[1] * secondary.shape[1])
    vmem, dma = pltpu.VMEM, pltpu.SemaphoreType.DMA
    shapes = (
        ((tokens.shape[0], head), bf16),
        (chunk, f32),
        (chunk, bf16),
        (chunk, bf16),
        ((1, blocks), f32),
        ((1, blocks), f32),
        (secondary.shape, bf16),
    )
    work = 4 * tokens.shape[0] * tokens.shape[1] * head
    outs = pl.pallas_call(
        functools.partial(step_kernel, limit),
        out_shape=[jax.ShapeDtypeStruct(shape, dtype) for shape, dtype in shapes],
        in_specs=[pl.BlockSpec(memory_space=pltpu.HBM)] * 8,
        out_specs=[pl.BlockSpec(memory_space=pltpu.HBM)] * 7,
        scratch_shapes=[
            *(vmem(shape, dtype) for shape, dtype in shapes),
            vmem(tokens.shape, bf16),
            vmem(cotangent.shape, bf16),
            vmem(secondary.shape, bf16),
            vmem(chunk, f32),
            vmem(chunk, bf16),
            vmem(chunk, bf16),
            vmem((1, blocks), f32),
            vmem((1, blocks), f32),
            vmem((4, 4) + chunk, bf16),
            vmem((4, 4) + chunk, bf16),
            vmem((2, 4) + chunk, bf16),
            vmem((2, 4) + chunk, bf16),
            vmem((4,) + chunk, f32),
            vmem((4,) + chunk, bf16),
            vmem((4,) + chunk, bf16),
            vmem((4,) + chunk, f32),
            vmem((3,) + chunk, bf16),
            vmem((3,) + chunk, bf16),
            vmem((4, 2, secondary.shape[0] // 2, head), bf16),
            vmem((3, 8, head), f32),
            vmem((7, 8, head), f32),
            vmem((2, 8, head), f32),
            vmem(chunk, f32),
            vmem(chunk, f32),
            dma((11,)),
            dma((14,)),
            dma((2, 16)),
            dma((2, 8)),
            dma((2, 4)),
            dma((2, 3)),
            dma((2, 3)),
            dma((2, 3)),
            dma((2, 3)),
            dma((2, 7)),
            dma((2, 3)),
            dma((2, 4)),
        ],
        compiler_params=pltpu.CompilerParams(
            collective_id=0, has_side_effects=True, vmem_limit_bytes=VMEM_BYTES
        ),
        cost_estimate=pl.CostEstimate(flops=work, bytes_accessed=8 << 20, transcendentals=0),
    )(
        tokens, cotangent, secondary, master, m_code, v_code,
        m_scale.reshape(1, blocks), v_scale.reshape(1, blocks),
    )
    outs = pl.pallas_call(
        write_kernel,
        out_shape=[jax.ShapeDtypeStruct(shape, dtype) for shape, dtype in shapes],
        in_specs=[pl.BlockSpec(memory_space=pltpu.HBM)] * 7,
        out_specs=[pl.BlockSpec(memory_space=pltpu.HBM)] * 7,
        scratch_shapes=[dma((7,))],
        compiler_params=pltpu.CompilerParams(vmem_limit_bytes=VMEM_BYTES),
    )(*outs)
    return (*outs[:4], outs[4].reshape(blocks), outs[5].reshape(blocks), outs[6])


def fits(mesh):
    return mesh.shape["outer"] == 8 and mesh.shape["inner"] == 4


def solution(mesh):
    in_specs = (
        P(("outer", "inner"), None),
        P(("outer", "inner"), None),
        P("inner", None),
        P(("inner", "outer"), None),
        P(("inner", "outer"), None),
        P(("inner", "outer"), None),
        P(("inner", "outer")),
        P(("inner", "outer")),
    )
    out_specs = (
        P(("outer", "inner"), None),
        P(("inner", "outer"), None),
        P(("inner", "outer"), None),
        P(("inner", "outer"), None),
        P(("inner", "outer")),
        P(("inner", "outer")),
        P("inner", None),
    )
    program = fused_body if fits(mesh) else body
    return jax.shard_map(
        program, mesh=mesh, in_specs=in_specs, out_specs=out_specs, check_vma=False
    )
```

```python
import functools
import math

import jax
import jax.numpy as jnp
from jax import lax
from jax.experimental import pallas as pl
from jax.experimental.pallas import tpu as pltpu
from jax.sharding import PartitionSpec as P

MESH = pl.DeviceIdType.MESH
PIECE = 128
VMEM_BYTES = 60 * 1024 * 1024
STEPS = (2, 1, 3, 0)


def adam_update(gradient, factor, master, m_code, v_code, m_scale, v_scale):
    blocks = m_scale.shape[0]
    height = master.shape[0] // blocks
    shaped = (blocks, height, master.shape[1])
    m_old = (m_code.astype(jnp.float32).reshape(shaped) * m_scale[:, None, None]).reshape(
        master.shape
    )
    v_old = (v_code.astype(jnp.float32).reshape(shaped) * v_scale[:, None, None]).reshape(
        master.shape
    )
    scaled = factor * gradient
    moment = 0.9 * m_old + 0.1 * scaled
    second = 0.95 * v_old + 0.05 * scaled * scaled
    master_new = master - 0.01 * (moment / (jnp.sqrt(second) + 1e-08) + 0.1 * master)
    moment_blocks = moment.reshape(blocks, -1)
    second_blocks = second.reshape(blocks, -1)
    m_scale_new = jnp.max(jnp.abs(moment_blocks), axis=1) + 1e-06
    v_scale_new = jnp.max(second_blocks, axis=1) + 1e-06
    m_code_new = (moment_blocks / m_scale_new[:, None]).reshape(master.shape).astype(jnp.bfloat16)
    v_code_new = (second_blocks / v_scale_new[:, None]).reshape(master.shape).astype(jnp.bfloat16)
    return (master_new, m_code_new, v_code_new, m_scale_new, v_scale_new)


def rounded_term(columns, cotangent):
    part = lax.dot_general(
        columns, cotangent, (((0,), (0,)), ((), ())), preferred_element_type=jnp.float32
    )
    part = lax.optimization_barrier(part.astype(jnp.bfloat16))
    return part.astype(jnp.float32)


def body(tokens, cotangent, secondary, master, m_code, v_code, m_scale, v_scale):
    tok_rows = tokens.shape[0]
    width = tokens.shape[1]
    n_outer = lax.axis_size("outer")
    n_inner = lax.axis_size("inner")
    columns = tokens
    projected = jnp.dot(
        columns,
        lax.all_gather(secondary, "inner", axis=0, tiled=True),
        preferred_element_type=jnp.float32,
    ).astype(jnp.bfloat16)
    reordered = (
        tokens.reshape(tok_rows, n_inner, n_outer, -1)
        .transpose(0, 2, 1, 3)
        .reshape(tok_rows, width)
    )
    columns = reordered
    gradient = lax.psum_scatter(
        rounded_term(columns, cotangent), ("outer", "inner"), scatter_dimension=0, tiled=True
    )
    total = lax.psum(jnp.sum(gradient * gradient), ("outer", "inner"))
    limit = 0.25 * math.sqrt(width * secondary.shape[1])
    factor = limit / jnp.maximum(jnp.sqrt(total), limit)
    master_new, m_code_new, v_code_new, m_scale_new, v_scale_new = adam_update(
        gradient, factor, master, m_code, v_code, m_scale, v_scale
    )
    secondary_new = lax.all_gather(master_new.astype(jnp.bfloat16), "outer", axis=0, tiled=True)
    return (projected, master_new, m_code_new, v_code_new, m_scale_new, v_scale_new, secondary_new)


def step_kernel(
    limit,
    tok_in, cot_in, sec_in, master_in, m_code_in, v_code_in, m_scale_in, v_scale_in,
    projected, master_new, m_code_new, v_code_new, m_scale_new, v_scale_new, sec_new,
    tok, cot, sec, master, m_code, v_code, m_scale, v_scale,
    send_a, recv_a, send_1, recv_1, sum_2, send_2, recv_2, sum_3, send_3, recv_3,
    weights, sq_1, sq_2, sq_send, moments, seconds,
    sem_in, sem_a, sem_1, sem_2, sem_3, sem_w, sem_f, sem_q1, sem_q2, sem_up, sem_down, sem_h,
):
    f32, bf16 = jnp.float32, jnp.bfloat16
    o, i = lax.axis_index("outer"), lax.axis_index("inner")
    n_z = 4
    core, z = o % 2, o // 2
    x, y = i % 2, i // 2
    to_x, to_y = i + 1 - 2 * x, i + 2 - 4 * y
    first = to_x * (1 - core) + to_y * core
    second = to_x * core + to_y * (1 - core)
    across = 3 - i
    mate = o + 1 - 2 * core
    rows = master.shape[0]
    half = sec.shape[0] // 2
    span = sec.shape[0]

    barrier = pltpu.get_barrier_semaphore()
    near = [(o, first), (o, second), (o, across)]
    far = [((o + d) % 8, i) for d in range(1, 8)]
    for peer in near + far:
        pl.semaphore_signal(barrier, inc=1, device_id=peer, device_id_type=MESH)

    loads = []

    def load(src, dst):
        loads.append(pltpu.make_async_copy(src, dst, sem_in.at[len(loads)]))
        loads[-1].start()

    load(cot_in, cot)
    for j in (across, second, first, i):
        columns = pl.ds(pl.multiple_of(j * span, 128), span)
        load(tok_in.at[:, columns], tok.at[:, columns])
    load(sec_in, sec)
    load(master_in, master)
    load(m_code_in, m_code)
    load(v_code_in, v_code)
    load(m_scale_in, m_scale)
    load(v_scale_in, v_scale)

    started = []

    def send(src, dst, sems, index, peer):
        copy = pltpu.make_async_remote_copy(
            src_ref=src, dst_ref=dst,
            send_sem=sems.at[0, index], recv_sem=sems.at[1, index],
            device_id=peer, device_id_type=MESH,
        )
        copy.start()
        started.append(copy)
        return copy

    def arrived(dst, sems, index):
        pltpu.make_async_remote_copy(
            src_ref=dst, dst_ref=dst,
            send_sem=sems.at[0, index], recv_sem=sems.at[1, index],
            device_id=(mate, i), device_id_type=MESH,
        ).wait_recv()

    def partial(j, s, c):
        block = j * 8 + ((z + STEPS[s]) % n_z) * 2 + c
        columns = tok[:, pl.ds(pl.multiple_of(block * rows, 128), rows)]
        return lax.dot_general(
            columns, cot[...], (((0,), (0,)), ((), ())), preferred_element_type=f32
        )

    mate_groups = (across, second, first, i)
    own_groups = (across, first, second, i)

    def for_mate(q):
        for s in range(4):
            send_a[q, s] = partial(mate_groups[q], s, 1 - core).astype(bf16)
            if q == 0 and s == 0:
                pl.semaphore_wait(barrier, 10)
            send(send_a.at[q, s], recv_a.at[q, s], sem_a, q * 4 + s, (mate, i))

    def chip_sum(q, s):
        own = partial(own_groups[q], s, core)
        arrived(recv_a.at[q, s], sem_a, q * 4 + s)
        return own + recv_a[q, s].astype(f32)

    def to_first(q):
        for s in range(4):
            send_1[q, s] = chip_sum(q, s).astype(bf16)
            send(send_1.at[q, s], recv_1.at[q, s], sem_1, q * 4 + s, (o, first))

    loads[0].wait()
    loads[1].wait()
    for_mate(0)
    loads[2].wait()
    for_mate(1)
    to_first(0)
    loads[3].wait()
    for_mate(2)
    to_first(1)
    loads[4].wait()
    for_mate(3)
    for s in range(4):
        sum_2[s] = chip_sum(2, s)
    for s in range(4):
        sum_3[s] = chip_sum(3, s)
    for s in range(4):
        arrived(recv_1.at[0, s], sem_1, s)
        send_2[s] = (sum_2[s] + recv_1[0, s].astype(f32)).astype(bf16)
        send(send_2.at[s], recv_2.at[s], sem_2, s, (o, second))

    for s in range(4):
        arrived(recv_1.at[1, s], sem_1, 4 + s)
        arrived(recv_2.at[s], sem_2, s)
        total = sum_3[s] + recv_1[1, s].astype(f32) + recv_2[s].astype(f32)
        if STEPS[s]:
            d = STEPS[s]
            send_3[d - 1] = total.astype(bf16)
            peer = ((z + d) % n_z) * 2 + core
            send(send_3.at[d - 1], recv_3.at[d - 1], sem_3, d - 1, (peer, i))
        else:
            sum_3[0] = total

    loads[5].wait()
    own_half = sec.at[pl.ds(pl.multiple_of(core * half, 128), half)]
    for index, peer in enumerate((first, second)):
        send(own_half, weights.at[i, core], sem_w, index, (o, peer))

    own_columns = tok[:, pl.ds(pl.multiple_of(i * span, 128), span)]
    out = jnp.dot(own_columns, sec[...], preferred_element_type=f32)

    for d in (1, 3, 2):
        arrived(recv_3.at[d - 1], sem_3, d - 1)
    gradient = sum_3[0]
    for d in range(1, 4):
        gradient = gradient + recv_3[d - 1].astype(f32)
    sum_3[0] = gradient

    squares = jnp.sum((gradient * gradient).reshape(rows // 8, 8, 128), axis=0)
    sq_send[0] = squares
    for index, peer in enumerate((first, second, across)):
        send(sq_send.at[0], sq_1.at[index], sem_q1, index, (o, peer))
    for index in range(3):
        arrived(sq_1.at[index], sem_q1, index)
        squares = squares + sq_1[index]
    sq_send[1] = squares
    for d in range(1, 8):
        send(sq_send.at[1], sq_2.at[d - 1], sem_q2, d - 1, ((o + d) % 8, i))

    for copy in loads[6:]:
        copy.wait()
    height = rows // m_scale.shape[1]

    def block_mask(p):
        shape = (PIECE, m_scale.shape[1])
        row = lax.broadcasted_iota(jnp.int32, shape, 0) + p * PIECE
        return row // height == lax.broadcasted_iota(jnp.int32, shape, 1)

    def expand(p, scales):
        return jnp.sum(jnp.where(block_mask(p), scales, 0.0), axis=1, keepdims=True)

    pieces = rows // PIECE
    for p in range(pieces):
        part = pl.ds(p * PIECE, PIECE)
        moments[part, :] = 0.9 * (m_code[part, :].astype(f32) * expand(p, m_scale[...]))
        seconds[part, :] = 0.95 * (v_code[part, :].astype(f32) * expand(p, v_scale[...]))

    for d in range(1, 8):
        arrived(sq_2.at[d - 1], sem_q2, d - 1)
        squares = squares + sq_2[d - 1]
    square_sum = jnp.sum(jnp.sum(squares, axis=0, keepdims=True), axis=1, keepdims=True)
    factor = limit / jnp.maximum(jnp.sqrt(square_sum), limit)

    for p in range(pieces):
        part = pl.ds(p * PIECE, PIECE)
        scaled = factor * sum_3[0, part, :]
        moment = moments[part, :] + 0.1 * scaled
        second_new = seconds[part, :] + 0.05 * scaled * scaled
        old = master[part, :]
        new = old - 0.01 * (moment / (jnp.sqrt(second_new) + 1e-08) + 0.1 * old)
        moments[part, :] = moment
        seconds[part, :] = second_new
        master_new[part, :] = new
        sec_new[pl.ds(pl.multiple_of(o * rows + p * PIECE, 128), PIECE), :] = new.astype(bf16)

    def new_rows(owner):
        return sec_new.at[pl.ds(pl.multiple_of(owner * rows, 128), rows)]

    relayed = []

    def relay(needed, owner, sems, index, peer):
        copy = pltpu.make_async_remote_copy(
            src_ref=new_rows(owner), dst_ref=new_rows(owner),
            send_sem=sems.at[0, index], recv_sem=sems.at[1, index],
            device_id=(peer, i), device_id_type=MESH,
        )
        pl.when(needed)(copy.start)
        relayed.append((needed, copy))

    def pass_on(t):
        for way, sems in ((1, sem_up), (-1, sem_down)):
            owner = o - 2 * t * way
            here = (z >= t) if way == 1 else (z + t < n_z)
            if t:
                pl.when(here)(functools.partial(arrived, new_rows(owner), sems, t - 1))
            if t < n_z - 1:
                more = here & ((z < n_z - 1) if way == 1 else (z > 0))
                relay(more, owner, sems, t, o + 2 * way)
            if t:
                relay(here, owner, sem_h, t if way == 1 else 3 + t, mate)

    def from_mate(t):
        for way in (1, -1):
            owner = mate - 2 * t * way
            here = (z >= t) if way == 1 else (z + t < n_z)
            pl.when(here)(functools.partial(arrived, new_rows(owner), sem_h, t if way == 1 else 3 + t))

    pass_on(0)
    send(new_rows(o), new_rows(o), sem_h, 0, (mate, i))

    arrived(weights.at[first, core], sem_w, 0)
    send(weights.at[first, core], weights.at[first, core], sem_w, 2, (o, second))
    send(weights.at[first, core], weights.at[first, core], sem_f, 0, (mate, i))
    arrived(weights.at[second, core], sem_w, 1)
    send(weights.at[second, core], weights.at[second, core], sem_f, 1, (mate, i))

    m_row = jnp.zeros(m_scale.shape, f32)
    v_row = jnp.zeros(v_scale.shape, f32)
    for p in range(pieces):
        part = pl.ds(p * PIECE, PIECE)
        mask = block_mask(p)
        for values, codes, is_m in ((moments, m_code_new, True), (seconds, v_code_new, False)):
            value = values[part, :]
            tops = jnp.max(jnp.abs(value), axis=1, keepdims=True)
            top = jnp.max(jnp.where(mask, tops, 0.0), axis=0, keepdims=True)
            scale = top + 1e-06
            codes[part, :] = (value / expand(p, scale)).astype(bf16)
            if is_m:
                m_row = jnp.maximum(m_row, top)
            else:
                v_row = jnp.maximum(v_row, top)
    m_scale_new[...] = m_row + 1e-06
    v_scale_new[...] = v_row + 1e-06

    def product(j, h):
        start = pl.multiple_of(j * span + h * half, 128)
        return jnp.dot(tok[:, pl.ds(start, half)], weights[j, h], preferred_element_type=f32)

    pass_on(1)
    out = out + product(first, core)
    out = out + product(second, core)
    pass_on(2)
    for index, j in enumerate((second, first)):
        arrived(weights.at[j, 1 - core], sem_f, index)
        out = out + product(j, 1 - core)
    arrived(weights.at[across, core], sem_w, 2)
    send(weights.at[across, core], weights.at[across, core], sem_f, 2, (mate, i))
    pass_on(3)
    out = out + product(across, core)
    arrived(weights.at[across, 1 - core], sem_f, 2)
    out = out + product(across, 1 - core)
    projected[...] = out.astype(bf16)
    arrived(new_rows(mate), sem_h, 0)
    for t in range(1, 4):
        from_mate(t)
    for needed, copy in relayed:
        pl.when(needed)(copy.wait_send)
    for copy in started:
        copy.wait_send()


def write_kernel(*refs):
    count = len(refs) // 2
    sems = refs[-1]
    copies = [
        pltpu.make_async_copy(refs[k], refs[count + k], sems.at[k]) for k in range(count)
    ]
    for copy in copies:
        copy.start()
    for copy in copies:
        copy.wait()


def fused_body(tokens, cotangent, secondary, master, m_code, v_code, m_scale, v_scale):
    f32, bf16 = jnp.float32, jnp.bfloat16
    rows, head = master.shape
    blocks = m_scale.shape[0]
    chunk = (rows, head)
    limit = 0.25 * math.sqrt(tokens.shape[1] * secondary.shape[1])
    vmem, dma = pltpu.VMEM, pltpu.SemaphoreType.DMA
    shapes = (
        ((tokens.shape[0], head), bf16),
        (chunk, f32),
        (chunk, bf16),
        (chunk, bf16),
        ((1, blocks), f32),
        ((1, blocks), f32),
        (secondary.shape, bf16),
    )
    work = 4 * tokens.shape[0] * tokens.shape[1] * head
    outs = pl.pallas_call(
        functools.partial(step_kernel, limit),
        out_shape=[vmem(shape, dtype) for shape, dtype in shapes],
        in_specs=[pl.BlockSpec(memory_space=pltpu.HBM)] * 8,
        out_specs=[pl.BlockSpec(memory_space=vmem)] * 7,
        scratch_shapes=[
            vmem(tokens.shape, bf16),
            vmem(cotangent.shape, bf16),
            vmem(secondary.shape, bf16),
            vmem(chunk, f32),
            vmem(chunk, bf16),
            vmem(chunk, bf16),
            vmem((1, blocks), f32),
            vmem((1, blocks), f32),
            vmem((4, 4) + chunk, bf16),
            vmem((4, 4) + chunk, bf16),
            vmem((2, 4) + chunk, bf16),
            vmem((2, 4) + chunk, bf16),
            vmem((4,) + chunk, f32),
            vmem((4,) + chunk, bf16),
            vmem((4,) + chunk, bf16),
            vmem((4,) + chunk, f32),
            vmem((3,) + chunk, bf16),
            vmem((3,) + chunk, bf16),
            vmem((4, 2, secondary.shape[0] // 2, head), bf16),
            vmem((3, 8, head), f32),
            vmem((7, 8, head), f32),
            vmem((2, 8, head), f32),
            vmem(chunk, f32),
            vmem(chunk, f32),
            dma((11,)),
            dma((2, 16)),
            dma((2, 8)),
            dma((2, 4)),
            dma((2, 3)),
            dma((2, 3)),
            dma((2, 3)),
            dma((2, 3)),
            dma((2, 7)),
            dma((2, 3)),
            dma((2, 3)),
            dma((2, 7)),
        ],
        compiler_params=pltpu.CompilerParams(
            collective_id=0, has_side_effects=True, vmem_limit_bytes=VMEM_BYTES
        ),
        cost_estimate=pl.CostEstimate(flops=work, bytes_accessed=8 << 20, transcendentals=0),
    )(
        tokens, cotangent, secondary, master, m_code, v_code,
        m_scale.reshape(1, blocks), v_scale.reshape(1, blocks),
    )
    outs = pl.pallas_call(
        write_kernel,
        out_shape=[jax.ShapeDtypeStruct(shape, dtype) for shape, dtype in shapes],
        in_specs=[pl.BlockSpec(memory_space=vmem)] * 7,
        out_specs=[pl.BlockSpec(memory_space=pltpu.HBM)] * 7,
        scratch_shapes=[dma((7,))],
        compiler_params=pltpu.CompilerParams(vmem_limit_bytes=VMEM_BYTES),
    )(*outs)
    return (*outs[:4], outs[4].reshape(blocks), outs[5].reshape(blocks), outs[6])


def fits(mesh):
    return mesh.shape["outer"] == 8 and mesh.shape["inner"] == 4


def solution(mesh):
    in_specs = (
        P(("outer", "inner"), None),
        P(("outer", "inner"), None),
        P("inner", None),
        P(("inner", "outer"), None),
        P(("inner", "outer"), None),
        P(("inner", "outer"), None),
        P(("inner", "outer")),
        P(("inner", "outer")),
    )
    out_specs = (
        P(("outer", "inner"), None),
        P(("inner", "outer"), None),
        P(("inner", "outer"), None),
        P(("inner", "outer"), None),
        P(("inner", "outer")),
        P(("inner", "outer")),
        P("inner", None),
    )
    program = fused_body if fits(mesh) else body
    return jax.shard_map(
        program, mesh=mesh, in_specs=in_specs, out_specs=out_specs, check_vma=False
    )
```

```python
import functools
import math

import jax
import jax.numpy as jnp
from jax import lax
from jax.experimental import pallas as pl
from jax.experimental.pallas import tpu as pltpu
from jax.sharding import PartitionSpec as P

MESH = pl.DeviceIdType.MESH
PIECE = 128
VMEM_BYTES = 60 * 1024 * 1024
STEPS = (2, 1, 3, 0)


def adam_update(gradient, factor, master, m_code, v_code, m_scale, v_scale):
    blocks = m_scale.shape[0]
    height = master.shape[0] // blocks
    shaped = (blocks, height, master.shape[1])
    m_old = (m_code.astype(jnp.float32).reshape(shaped) * m_scale[:, None, None]).reshape(
        master.shape
    )
    v_old = (v_code.astype(jnp.float32).reshape(shaped) * v_scale[:, None, None]).reshape(
        master.shape
    )
    scaled = factor * gradient
    moment = 0.9 * m_old + 0.1 * scaled
    second = 0.95 * v_old + 0.05 * scaled * scaled
    master_new = master - 0.01 * (moment / (jnp.sqrt(second) + 1e-08) + 0.1 * master)
    moment_blocks = moment.reshape(blocks, -1)
    second_blocks = second.reshape(blocks, -1)
    m_scale_new = jnp.max(jnp.abs(moment_blocks), axis=1) + 1e-06
    v_scale_new = jnp.max(second_blocks, axis=1) + 1e-06
    m_code_new = (moment_blocks / m_scale_new[:, None]).reshape(master.shape).astype(jnp.bfloat16)
    v_code_new = (second_blocks / v_scale_new[:, None]).reshape(master.shape).astype(jnp.bfloat16)
    return (master_new, m_code_new, v_code_new, m_scale_new, v_scale_new)


def rounded_term(columns, cotangent):
    part = lax.dot_general(
        columns, cotangent, (((0,), (0,)), ((), ())), preferred_element_type=jnp.float32
    )
    part = lax.optimization_barrier(part.astype(jnp.bfloat16))
    return part.astype(jnp.float32)


def body(tokens, cotangent, secondary, master, m_code, v_code, m_scale, v_scale):
    tok_rows = tokens.shape[0]
    width = tokens.shape[1]
    n_outer = lax.axis_size("outer")
    n_inner = lax.axis_size("inner")
    columns = tokens
    projected = jnp.dot(
        columns,
        lax.all_gather(secondary, "inner", axis=0, tiled=True),
        preferred_element_type=jnp.float32,
    ).astype(jnp.bfloat16)
    reordered = (
        tokens.reshape(tok_rows, n_inner, n_outer, -1)
        .transpose(0, 2, 1, 3)
        .reshape(tok_rows, width)
    )
    columns = reordered
    gradient = lax.psum_scatter(
        rounded_term(columns, cotangent), ("outer", "inner"), scatter_dimension=0, tiled=True
    )
    total = lax.psum(jnp.sum(gradient * gradient), ("outer", "inner"))
    limit = 0.25 * math.sqrt(width * secondary.shape[1])
    factor = limit / jnp.maximum(jnp.sqrt(total), limit)
    master_new, m_code_new, v_code_new, m_scale_new, v_scale_new = adam_update(
        gradient, factor, master, m_code, v_code, m_scale, v_scale
    )
    secondary_new = lax.all_gather(master_new.astype(jnp.bfloat16), "outer", axis=0, tiled=True)
    return (projected, master_new, m_code_new, v_code_new, m_scale_new, v_scale_new, secondary_new)


def step_kernel(
    limit,
    tok_in, cot_in, sec_in, master_in, m_code_in, v_code_in, m_scale_in, v_scale_in,
    projected, master_new, m_code_new, v_code_new, m_scale_new, v_scale_new, sec_new,
    tok, cot, sec, master, m_code, v_code, m_scale, v_scale,
    send_a, recv_a, send_1, recv_1, send_2, recv_2, sum_3, send_3, recv_3,
    weights, sq_1, sq_2, sq_send, moments, seconds,
    sem_in, sem_a, sem_1, sem_2, sem_3, sem_w, sem_f, sem_q1, sem_q2, sem_g, sem_h,
):
    f32, bf16 = jnp.float32, jnp.bfloat16
    o, i = lax.axis_index("outer"), lax.axis_index("inner")
    n_z = 4
    core, z = o % 2, o // 2
    x, y = i % 2, i // 2
    to_x, to_y = i + 1 - 2 * x, i + 2 - 4 * y
    first = to_x * (1 - core) + to_y * core
    second = to_x * core + to_y * (1 - core)
    across = 3 - i
    mate = o + 1 - 2 * core
    rows = master.shape[0]
    half = sec.shape[0] // 2
    span = sec.shape[0]

    barrier = pltpu.get_barrier_semaphore()
    near = [(o, first), (o, second), (o, across)]
    far = [((o + d) % 8, i) for d in range(1, 8)]
    for peer in near + far:
        pl.semaphore_signal(barrier, inc=1, device_id=peer, device_id_type=MESH)

    loads = []

    def load(src, dst):
        loads.append(pltpu.make_async_copy(src, dst, sem_in.at[len(loads)]))
        loads[-1].start()

    load(cot_in, cot)
    groups = (across, second, first, i)
    for j in groups[:2]:
        columns = pl.ds(pl.multiple_of(j * span, 128), span)
        load(tok_in.at[:, columns], tok.at[:, columns])
    load(sec_in, sec)
    for j in groups[2:]:
        columns = pl.ds(pl.multiple_of(j * span, 128), span)
        load(tok_in.at[:, columns], tok.at[:, columns])
    load(master_in, master)
    load(m_code_in, m_code)
    load(v_code_in, v_code)
    load(m_scale_in, m_scale)
    load(v_scale_in, v_scale)

    started = []

    def send(src, dst, sems, index, peer):
        copy = pltpu.make_async_remote_copy(
            src_ref=src, dst_ref=dst,
            send_sem=sems.at[0, index], recv_sem=sems.at[1, index],
            device_id=peer, device_id_type=MESH,
        )
        copy.start()
        started.append(copy)
        return copy

    def arrived(dst, sems, index):
        pltpu.make_async_remote_copy(
            src_ref=dst, dst_ref=dst,
            send_sem=sems.at[0, index], recv_sem=sems.at[1, index],
            device_id=(mate, i), device_id_type=MESH,
        ).wait_recv()

    def weight_part(j, part):
        third = half // 3
        return weights.at[j, core, pl.ds(part * third, third + part * third)]

    def send_weights(part):
        third = half // 3
        start = pl.multiple_of(core * half + part * third, 128)
        source = sec.at[pl.ds(start, third + part * third)]
        for index, peer in enumerate((first, second)):
            send(source, weight_part(i, part), sem_w, 2 * part + index, (o, peer))

    def for_both(g):
        base = groups[g] * span
        for k in range(n_z):
            for c in range(2):
                start = pl.multiple_of(base + (k * 2 + c) * rows, 128)
                part = lax.dot_general(
                    tok[:, pl.ds(start, rows)], cot[...], (((0,), (0,)), ((), ())),
                    preferred_element_type=f32,
                )
                send_a[g, c, k] = part.astype(bf16)

    def to_mate(g):
        send(send_a.at[g, 1 - core], recv_a.at[g], sem_a, g, (mate, i))

    def chip_sum(q, s):
        k = (z + STEPS[s]) % n_z
        own = send_a[(0, 2, 1, 3)[q], core, k]
        return own.astype(f32) + recv_a[q, k].astype(f32)

    def to_first(q):
        arrived(recv_a.at[q], sem_a, q)
        for s in range(4):
            send_1[q, s] = chip_sum(q, s).astype(bf16)
            send(send_1.at[q, s], recv_1.at[q, s], sem_1, q * 4 + s, (o, first))

    loads[0].wait()
    loads[1].wait()
    for_both(0)
    pl.semaphore_wait(barrier, 10)
    to_mate(0)
    loads[3].wait()
    send_weights(0)
    loads[2].wait()
    for_both(1)
    to_mate(1)
    to_first(0)
    loads[4].wait()
    for_both(2)
    to_mate(2)
    to_first(1)
    loads[5].wait()
    for_both(3)
    to_mate(3)
    arrived(recv_a.at[2], sem_a, 2)
    for s in range(4):
        arrived(recv_1.at[0, s], sem_1, s)
        send_2[s] = (chip_sum(2, s) + recv_1[0, s].astype(f32)).astype(bf16)
        send(send_2.at[s], recv_2.at[s], sem_2, s, (o, second))
    arrived(recv_a.at[3], sem_a, 3)
    for s in range(4):
        sum_3[s] = chip_sum(3, s)

    for s in range(4):
        arrived(recv_1.at[1, s], sem_1, 4 + s)
        arrived(recv_2.at[s], sem_2, s)
        total = sum_3[s] + recv_1[1, s].astype(f32) + recv_2[s].astype(f32)
        if STEPS[s]:
            d = STEPS[s]
            send_3[d - 1] = total.astype(bf16)
            peer = ((z + d) % n_z) * 2 + core
            send(send_3.at[d - 1], recv_3.at[d - 1], sem_3, d - 1, (peer, i))
        else:
            sum_3[0] = total

    send_weights(1)
    arrived(weight_part(first, 0), sem_w, 0)
    send(weight_part(first, 0), weight_part(first, 0), sem_w, 4, (o, second))
    arrived(weight_part(second, 0), sem_w, 1)

    own_columns = tok[:, pl.ds(pl.multiple_of(i * span, 128), span)]
    out = jnp.dot(own_columns, sec[...], preferred_element_type=f32)

    for d in (1, 3, 2):
        arrived(recv_3.at[d - 1], sem_3, d - 1)
    gradient = sum_3[0]
    for d in range(1, 4):
        gradient = gradient + recv_3[d - 1].astype(f32)
    sum_3[0] = gradient

    squares = jnp.sum((gradient * gradient).reshape(rows // 8, 8, 128), axis=0)
    sq_send[0] = squares
    for d in range(1, 8):
        send(sq_send.at[0], sq_2.at[d - 1], sem_q2, d - 1, ((o + d) % 8, i))
    for copy in loads[6:]:
        copy.wait()
    height = rows // m_scale.shape[1]

    def block_mask(p):
        shape = (PIECE, m_scale.shape[1])
        row = lax.broadcasted_iota(jnp.int32, shape, 0) + p * PIECE
        return row // height == lax.broadcasted_iota(jnp.int32, shape, 1)

    def expand(p, scales):
        return jnp.sum(jnp.where(block_mask(p), scales, 0.0), axis=1, keepdims=True)

    pieces = rows // PIECE
    for p in range(pieces):
        part = pl.ds(p * PIECE, PIECE)
        moments[part, :] = 0.9 * (m_code[part, :].astype(f32) * expand(p, m_scale[...]))
        seconds[part, :] = 0.95 * (v_code[part, :].astype(f32) * expand(p, v_scale[...]))

    for d in range(1, 8):
        arrived(sq_2.at[d - 1], sem_q2, d - 1)
        squares = squares + sq_2[d - 1]
    sq_send[1] = squares
    for index, peer in enumerate((first, second, across)):
        send(sq_send.at[1], sq_1.at[index], sem_q1, index, (o, peer))
    for index in range(3):
        arrived(sq_1.at[index], sem_q1, index)
        squares = squares + sq_1[index]
    square_sum = jnp.sum(jnp.sum(squares, axis=0, keepdims=True), axis=1, keepdims=True)
    factor = limit / jnp.maximum(jnp.sqrt(square_sum), limit)

    for p in range(pieces):
        part = pl.ds(p * PIECE, PIECE)
        scaled = factor * sum_3[0, part, :]
        moment = moments[part, :] + 0.1 * scaled
        second_new = seconds[part, :] + 0.05 * scaled * scaled
        old = master[part, :]
        new = old - 0.01 * (moment / (jnp.sqrt(second_new) + 1e-08) + 0.1 * old)
        moments[part, :] = moment
        seconds[part, :] = second_new
        master_new[part, :] = new
        sec_new[pl.ds(pl.multiple_of(o * rows + p * PIECE, 128), PIECE), :] = new.astype(bf16)

    def new_rows(owner):
        return sec_new.at[pl.ds(pl.multiple_of(owner * rows, 128), rows)]

    for d in (2, 1, 3):
        send(new_rows(o), new_rows(o), sem_g, d - 1, (((z + d) % n_z) * 2 + core, i))
    send(new_rows(o), new_rows(o), sem_h, 0, (mate, i))

    arrived(weight_part(first, 1), sem_w, 2)
    send(weight_part(first, 1), weight_part(first, 1), sem_w, 5, (o, second))
    send(weights.at[first, core], weights.at[first, core], sem_f, 0, (mate, i))
    arrived(weight_part(second, 1), sem_w, 3)
    send(weights.at[second, core], weights.at[second, core], sem_f, 1, (mate, i))

    m_row = jnp.zeros(m_scale.shape, f32)
    v_row = jnp.zeros(v_scale.shape, f32)
    for p in range(pieces):
        part = pl.ds(p * PIECE, PIECE)
        mask = block_mask(p)
        for values, codes, is_m in ((moments, m_code_new, True), (seconds, v_code_new, False)):
            value = values[part, :]
            tops = jnp.max(jnp.abs(value), axis=1, keepdims=True)
            top = jnp.max(jnp.where(mask, tops, 0.0), axis=0, keepdims=True)
            scale = top + 1e-06
            codes[part, :] = (value / expand(p, scale)).astype(bf16)
            if is_m:
                m_row = jnp.maximum(m_row, top)
            else:
                v_row = jnp.maximum(v_row, top)
    m_scale_new[...] = m_row + 1e-06
    v_scale_new[...] = v_row + 1e-06

    def product(j, h):
        start = pl.multiple_of(j * span + h * half, 128)
        return jnp.dot(tok[:, pl.ds(start, half)], weights[j, h], preferred_element_type=f32)

    def gathered(d):
        owner = ((z + n_z - d) % n_z) * 2 + core
        arrived(new_rows(owner), sem_g, d - 1)
        send(new_rows(owner), new_rows(owner), sem_h, d, (mate, i))

    out = out + product(first, core)
    out = out + product(second, core)
    gathered(1)
    arrived(weight_part(across, 0), sem_w, 4)
    arrived(weight_part(across, 1), sem_w, 5)
    send(weights.at[across, core], weights.at[across, core], sem_f, 2, (mate, i))
    out = out + product(across, core)
    gathered(3)
    for index, j in enumerate((second, first)):
        arrived(weights.at[j, 1 - core], sem_f, index)
        out = out + product(j, 1 - core)
    gathered(2)
    arrived(weights.at[across, 1 - core], sem_f, 2)
    out = out + product(across, 1 - core)
    projected[...] = out.astype(bf16)
    for d in range(4):
        owner = ((z + n_z - d) % n_z) * 2 + 1 - core
        arrived(new_rows(owner), sem_h, d)
    for copy in started:
        copy.wait_send()


def write_kernel(*refs):
    count = len(refs) // 2
    sems = refs[-1]
    copies = [
        pltpu.make_async_copy(refs[k], refs[count + k], sems.at[k]) for k in range(count)
    ]
    for copy in copies:
        copy.start()
    for copy in copies:
        copy.wait()


def fused_body(tokens, cotangent, secondary, master, m_code, v_code, m_scale, v_scale):
    f32, bf16 = jnp.float32, jnp.bfloat16
    rows, head = master.shape
    blocks = m_scale.shape[0]
    chunk = (rows, head)
    limit = 0.25 * math.sqrt(tokens.shape[1] * secondary.shape[1])
    vmem, dma = pltpu.VMEM, pltpu.SemaphoreType.DMA
    shapes = (
        ((tokens.shape[0], head), bf16),
        (chunk, f32),
        (chunk, bf16),
        (chunk, bf16),
        ((1, blocks), f32),
        ((1, blocks), f32),
        (secondary.shape, bf16),
    )
    work = 4 * tokens.shape[0] * tokens.shape[1] * head
    outs = pl.pallas_call(
        functools.partial(step_kernel, limit),
        out_shape=[vmem(shape, dtype) for shape, dtype in shapes],
        in_specs=[pl.BlockSpec(memory_space=pltpu.HBM)] * 8,
        out_specs=[pl.BlockSpec(memory_space=vmem)] * 7,
        scratch_shapes=[
            vmem(tokens.shape, bf16),
            vmem(cotangent.shape, bf16),
            vmem(secondary.shape, bf16),
            vmem(chunk, f32),
            vmem(chunk, bf16),
            vmem(chunk, bf16),
            vmem((1, blocks), f32),
            vmem((1, blocks), f32),
            vmem((4, 2, 4) + chunk, bf16),
            vmem((4, 4) + chunk, bf16),
            vmem((2, 4) + chunk, bf16),
            vmem((2, 4) + chunk, bf16),
            vmem((4,) + chunk, bf16),
            vmem((4,) + chunk, bf16),
            vmem((4,) + chunk, f32),
            vmem((3,) + chunk, bf16),
            vmem((3,) + chunk, bf16),
            vmem((4, 2, secondary.shape[0] // 2, head), bf16),
            vmem((3, 8, head), f32),
            vmem((7, 8, head), f32),
            vmem((2, 8, head), f32),
            vmem(chunk, f32),
            vmem(chunk, f32),
            dma((11,)),
            dma((2, 4)),
            dma((2, 8)),
            dma((2, 4)),
            dma((2, 3)),
            dma((2, 6)),
            dma((2, 3)),
            dma((2, 3)),
            dma((2, 7)),
            dma((2, 3)),
            dma((2, 4)),
        ],
        compiler_params=pltpu.CompilerParams(
            collective_id=0, has_side_effects=True, vmem_limit_bytes=VMEM_BYTES
        ),
        cost_estimate=pl.CostEstimate(flops=work, bytes_accessed=8 << 20, transcendentals=0),
    )(
        tokens, cotangent, secondary, master, m_code, v_code,
        m_scale.reshape(1, blocks), v_scale.reshape(1, blocks),
    )
    outs = pl.pallas_call(
        write_kernel,
        out_shape=[jax.ShapeDtypeStruct(shape, dtype) for shape, dtype in shapes],
        in_specs=[pl.BlockSpec(memory_space=vmem)] * 7,
        out_specs=[pl.BlockSpec(memory_space=pltpu.HBM)] * 7,
        scratch_shapes=[dma((7,))],
        compiler_params=pltpu.CompilerParams(vmem_limit_bytes=4 << 20),
    )(*outs)
    return (*outs[:4], outs[4].reshape(blocks), outs[5].reshape(blocks), outs[6])


def fits(mesh):
    return mesh.shape["outer"] == 8 and mesh.shape["inner"] == 4


def solution(mesh):
    in_specs = (
        P(("outer", "inner"), None),
        P(("outer", "inner"), None),
        P("inner", None),
        P(("inner", "outer"), None),
        P(("inner", "outer"), None),
        P(("inner", "outer"), None),
        P(("inner", "outer")),
        P(("inner", "outer")),
    )
    out_specs = (
        P(("outer", "inner"), None),
        P(("inner", "outer"), None),
        P(("inner", "outer"), None),
        P(("inner", "outer"), None),
        P(("inner", "outer")),
        P(("inner", "outer")),
        P("inner", None),
    )
    program = fused_body if fits(mesh) else body
    return jax.shard_map(
        program, mesh=mesh, in_specs=in_specs, out_specs=out_specs, check_vma=False
    )
```

```python
import functools
import math

import jax
import jax.numpy as jnp
from jax import lax
from jax.experimental import pallas as pl
from jax.experimental.pallas import tpu as pltpu
from jax.sharding import PartitionSpec as P

MESH = pl.DeviceIdType.MESH
PIECE = 128
VMEM_BYTES = 60 * 1024 * 1024
STEPS = (2, 1, 3, 0)


def adam_update(gradient, factor, master, m_code, v_code, m_scale, v_scale):
    blocks = m_scale.shape[0]
    height = master.shape[0] // blocks
    shaped = (blocks, height, master.shape[1])
    m_old = (m_code.astype(jnp.float32).reshape(shaped) * m_scale[:, None, None]).reshape(
        master.shape
    )
    v_old = (v_code.astype(jnp.float32).reshape(shaped) * v_scale[:, None, None]).reshape(
        master.shape
    )
    scaled = factor * gradient
    moment = 0.9 * m_old + 0.1 * scaled
    second = 0.95 * v_old + 0.05 * scaled * scaled
    master_new = master - 0.01 * (moment / (jnp.sqrt(second) + 1e-08) + 0.1 * master)
    moment_blocks = moment.reshape(blocks, -1)
    second_blocks = second.reshape(blocks, -1)
    m_scale_new = jnp.max(jnp.abs(moment_blocks), axis=1) + 1e-06
    v_scale_new = jnp.max(second_blocks, axis=1) + 1e-06
    m_code_new = (moment_blocks / m_scale_new[:, None]).reshape(master.shape).astype(jnp.bfloat16)
    v_code_new = (second_blocks / v_scale_new[:, None]).reshape(master.shape).astype(jnp.bfloat16)
    return (master_new, m_code_new, v_code_new, m_scale_new, v_scale_new)


def rounded_term(columns, cotangent):
    part = lax.dot_general(
        columns, cotangent, (((0,), (0,)), ((), ())), preferred_element_type=jnp.float32
    )
    part = lax.optimization_barrier(part.astype(jnp.bfloat16))
    return part.astype(jnp.float32)


def body(tokens, cotangent, secondary, master, m_code, v_code, m_scale, v_scale):
    tok_rows = tokens.shape[0]
    width = tokens.shape[1]
    n_outer = lax.axis_size("outer")
    n_inner = lax.axis_size("inner")
    columns = tokens
    projected = jnp.dot(
        columns,
        lax.all_gather(secondary, "inner", axis=0, tiled=True),
        preferred_element_type=jnp.float32,
    ).astype(jnp.bfloat16)
    reordered = (
        tokens.reshape(tok_rows, n_inner, n_outer, -1)
        .transpose(0, 2, 1, 3)
        .reshape(tok_rows, width)
    )
    columns = reordered
    gradient = lax.psum_scatter(
        rounded_term(columns, cotangent), ("outer", "inner"), scatter_dimension=0, tiled=True
    )
    total = lax.psum(jnp.sum(gradient * gradient), ("outer", "inner"))
    limit = 0.25 * math.sqrt(width * secondary.shape[1])
    factor = limit / jnp.maximum(jnp.sqrt(total), limit)
    master_new, m_code_new, v_code_new, m_scale_new, v_scale_new = adam_update(
        gradient, factor, master, m_code, v_code, m_scale, v_scale
    )
    secondary_new = lax.all_gather(master_new.astype(jnp.bfloat16), "outer", axis=0, tiled=True)
    return (projected, master_new, m_code_new, v_code_new, m_scale_new, v_scale_new, secondary_new)


def step_kernel(
    limit,
    tok_in, cot_in, sec_in, master_in, m_code_in, v_code_in, m_scale_in, v_scale_in,
    projected, master_new, m_code_new, v_code_new, m_scale_new, v_scale_new, sec_new,
    tok, cot, sec, master, m_code, v_code, m_scale, v_scale,
    send_a, recv_a, send_1, recv_1, send_2, recv_2, sum_3, send_3, recv_3,
    weights, sq_1, sq_2, sq_send, moments, seconds,
    sem_in, sem_a, sem_1, sem_2, sem_3, sem_w, sem_f, sem_q1, sem_q2, sem_g, sem_h,
):
    f32, bf16 = jnp.float32, jnp.bfloat16
    o, i = lax.axis_index("outer"), lax.axis_index("inner")
    n_z = 4
    core, z = o % 2, o // 2
    x, y = i % 2, i // 2
    to_x, to_y = i + 1 - 2 * x, i + 2 - 4 * y
    first = to_x * (1 - core) + to_y * core
    second = to_x * core + to_y * (1 - core)
    across = 3 - i
    mate = o + 1 - 2 * core
    rows = master.shape[0]
    half = sec.shape[0] // 2
    span = sec.shape[0]

    barrier = pltpu.get_barrier_semaphore()
    near = [(o, first), (o, second), (o, across)]
    far = [((o + d) % 8, i) for d in range(1, 8)]
    for peer in near + far:
        pl.semaphore_signal(barrier, inc=1, device_id=peer, device_id_type=MESH)

    loads = []

    def load(src, dst):
        loads.append(pltpu.make_async_copy(src, dst, sem_in.at[len(loads)]))
        loads[-1].start()

    load(cot_in, cot)
    groups = (across, second, first, i)
    pair = 2 * rows

    def columns_of(g, s):
        start = groups[g] * span + ((z + STEPS[s]) % n_z) * pair
        return pl.multiple_of(start, 128)

    for s in range(4):
        for g in range(4):
            columns = pl.ds(columns_of(g, s), pair)
            load(tok_in.at[:, columns], tok.at[:, columns])
        if s == 0:
            load(sec_in, sec)
    load(master_in, master)
    load(m_code_in, m_code)
    load(v_code_in, v_code)
    load(m_scale_in, m_scale)
    load(v_scale_in, v_scale)

    started = []

    def send(src, dst, sems, index, peer):
        copy = pltpu.make_async_remote_copy(
            src_ref=src, dst_ref=dst,
            send_sem=sems.at[0, index], recv_sem=sems.at[1, index],
            device_id=peer, device_id_type=MESH,
        )
        copy.start()
        started.append(copy)
        return copy

    def arrived(dst, sems, index):
        pltpu.make_async_remote_copy(
            src_ref=dst, dst_ref=dst,
            send_sem=sems.at[0, index], recv_sem=sems.at[1, index],
            device_id=(mate, i), device_id_type=MESH,
        ).wait_recv()

    def weight_part(j, part):
        third = half // 3
        return weights.at[j, core, pl.ds(part * third, third + part * third)]

    def send_weights(part):
        third = half // 3
        start = pl.multiple_of(core * half + part * third, 128)
        source = sec.at[pl.ds(start, third + part * third)]
        for index, peer in enumerate((first, second)):
            send(source, weight_part(i, part), sem_w, 2 * part + index, (o, peer))

    def for_both(s):
        for g in range(4):
            loads[1 + 4 * s + g + (s > 0)].wait()
        for g in range(4):
            for c in range(2):
                start = pl.multiple_of(columns_of(g, s) + c * rows, 128)
                part = lax.dot_general(
                    tok[:, pl.ds(start, rows)], cot[...], (((0,), (0,)), ((), ())),
                    preferred_element_type=f32,
                )
                send_a[s, c, g] = part.astype(bf16)

    def to_mate(s):
        send(send_a.at[s, 1 - core], recv_a.at[s], sem_a, s, (mate, i))

    def chip_sum(q, s):
        own = send_a[s, core, (0, 2, 1, 3)[q]]
        return own.astype(f32) + recv_a[s, q].astype(f32)

    def to_first(s):
        arrived(recv_a.at[s], sem_a, s)
        for q in range(2):
            send_1[q, s] = chip_sum(q, s).astype(bf16)
            send(send_1.at[q, s], recv_1.at[q, s], sem_1, q * 4 + s, (o, first))

    def to_second(s):
        arrived(recv_1.at[0, s], sem_1, s)
        send_2[s] = (chip_sum(2, s) + recv_1[0, s].astype(f32)).astype(bf16)
        send(send_2.at[s], recv_2.at[s], sem_2, s, (o, second))

    def along_z(s):
        arrived(recv_1.at[1, s], sem_1, 4 + s)
        arrived(recv_2.at[s], sem_2, s)
        total = chip_sum(3, s) + recv_1[1, s].astype(f32) + recv_2[s].astype(f32)
        if STEPS[s]:
            d = STEPS[s]
            send_3[d - 1] = total.astype(bf16)
            peer = ((z + d) % n_z) * 2 + core
            send(send_3.at[d - 1], recv_3.at[d - 1], sem_3, d - 1, (peer, i))
        else:
            sum_3[...] = total

    loads[0].wait()
    for_both(0)
    pl.semaphore_wait(barrier, 10)
    to_mate(0)
    loads[5].wait()
    send_weights(0)
    for_both(1)
    to_mate(1)
    to_first(0)
    for_both(2)
    to_mate(2)
    to_first(1)
    for_both(3)
    to_mate(3)
    to_second(0)
    to_first(2)
    to_second(1)
    to_first(3)
    along_z(0)
    to_second(2)
    along_z(1)
    to_second(3)
    along_z(2)
    along_z(3)

    send_weights(1)
    arrived(weight_part(first, 0), sem_w, 0)
    send(weight_part(first, 0), weight_part(first, 0), sem_w, 4, (o, second))
    arrived(weight_part(second, 0), sem_w, 1)

    own_columns = tok[:, pl.ds(pl.multiple_of(i * span, 128), span)]
    out = jnp.dot(own_columns, sec[...], preferred_element_type=f32)

    for d in (1, 3, 2):
        arrived(recv_3.at[d - 1], sem_3, d - 1)
    gradient = sum_3[...]
    for d in range(1, 4):
        gradient = gradient + recv_3[d - 1].astype(f32)
    sum_3[...] = gradient

    squares = jnp.sum((gradient * gradient).reshape(rows // 8, 8, 128), axis=0)
    sq_send[0] = squares
    for d in range(1, 8):
        send(sq_send.at[0], sq_2.at[d - 1], sem_q2, d - 1, ((o + d) % 8, i))
    for copy in loads[18:]:
        copy.wait()
    height = rows // m_scale.shape[1]

    def block_mask(p):
        shape = (PIECE, m_scale.shape[1])
        row = lax.broadcasted_iota(jnp.int32, shape, 0) + p * PIECE
        return row // height == lax.broadcasted_iota(jnp.int32, shape, 1)

    def expand(p, scales):
        return jnp.sum(jnp.where(block_mask(p), scales, 0.0), axis=1, keepdims=True)

    pieces = rows // PIECE
    for p in range(pieces):
        part = pl.ds(p * PIECE, PIECE)
        moments[part, :] = 0.9 * (m_code[part, :].astype(f32) * expand(p, m_scale[...]))
        seconds[part, :] = 0.95 * (v_code[part, :].astype(f32) * expand(p, v_scale[...]))

    for d in range(1, 8):
        arrived(sq_2.at[d - 1], sem_q2, d - 1)
        squares = squares + sq_2[d - 1]
    sq_send[1] = squares
    for index, peer in enumerate((first, second, across)):
        send(sq_send.at[1], sq_1.at[index], sem_q1, index, (o, peer))
    for index in range(3):
        arrived(sq_1.at[index], sem_q1, index)
        squares = squares + sq_1[index]
    square_sum = jnp.sum(jnp.sum(squares, axis=0, keepdims=True), axis=1, keepdims=True)
    factor = limit / jnp.maximum(jnp.sqrt(square_sum), limit)

    for p in range(pieces):
        part = pl.ds(p * PIECE, PIECE)
        scaled = factor * sum_3[part, :]
        moment = moments[part, :] + 0.1 * scaled
        second_new = seconds[part, :] + 0.05 * scaled * scaled
        old = master[part, :]
        new = old - 0.01 * (moment / (jnp.sqrt(second_new) + 1e-08) + 0.1 * old)
        moments[part, :] = moment
        seconds[part, :] = second_new
        master_new[part, :] = new
        sec_new[pl.ds(pl.multiple_of(o * rows + p * PIECE, 128), PIECE), :] = new.astype(bf16)

    def new_rows(owner):
        return sec_new.at[pl.ds(pl.multiple_of(owner * rows, 128), rows)]

    for d in (2, 1, 3):
        send(new_rows(o), new_rows(o), sem_g, d - 1, (((z + d) % n_z) * 2 + core, i))
    send(new_rows(o), new_rows(o), sem_h, 0, (mate, i))

    arrived(weight_part(first, 1), sem_w, 2)
    send(weight_part(first, 1), weight_part(first, 1), sem_w, 5, (o, second))
    send(weights.at[first, core], weights.at[first, core], sem_f, 0, (mate, i))
    arrived(weight_part(second, 1), sem_w, 3)
    send(weights.at[second, core], weights.at[second, core], sem_f, 1, (mate, i))

    m_row = jnp.zeros(m_scale.shape, f32)
    v_row = jnp.zeros(v_scale.shape, f32)
    for p in range(pieces):
        part = pl.ds(p * PIECE, PIECE)
        mask = block_mask(p)
        for values, codes, is_m in ((moments, m_code_new, True), (seconds, v_code_new, False)):
            value = values[part, :]
            tops = jnp.max(jnp.abs(value), axis=1, keepdims=True)
            top = jnp.max(jnp.where(mask, tops, 0.0), axis=0, keepdims=True)
            scale = top + 1e-06
            codes[part, :] = (value / expand(p, scale)).astype(bf16)
            if is_m:
                m_row = jnp.maximum(m_row, top)
            else:
                v_row = jnp.maximum(v_row, top)
    m_scale_new[...] = m_row + 1e-06
    v_scale_new[...] = v_row + 1e-06

    def product(j, h):
        start = pl.multiple_of(j * span + h * half, 128)
        return jnp.dot(tok[:, pl.ds(start, half)], weights[j, h], preferred_element_type=f32)

    def gathered(d):
        owner = ((z + n_z - d) % n_z) * 2 + core
        arrived(new_rows(owner), sem_g, d - 1)
        send(new_rows(owner), new_rows(owner), sem_h, d, (mate, i))

    out = out + product(first, core)
    out = out + product(second, core)
    gathered(1)
    arrived(weight_part(across, 0), sem_w, 4)
    arrived(weight_part(across, 1), sem_w, 5)
    send(weights.at[across, core], weights.at[across, core], sem_f, 2, (mate, i))
    out = out + product(across, core)
    gathered(3)
    for index, j in enumerate((second, first)):
        arrived(weights.at[j, 1 - core], sem_f, index)
        out = out + product(j, 1 - core)
    gathered(2)
    arrived(weights.at[across, 1 - core], sem_f, 2)
    out = out + product(across, 1 - core)
    projected[...] = out.astype(bf16)
    for d in range(4):
        owner = ((z + n_z - d) % n_z) * 2 + 1 - core
        arrived(new_rows(owner), sem_h, d)
    for copy in started:
        copy.wait_send()


def write_kernel(*refs):
    count = len(refs) // 2
    sems = refs[-1]
    copies = [
        pltpu.make_async_copy(refs[k], refs[count + k], sems.at[k]) for k in range(count)
    ]
    for copy in copies:
        copy.start()
    for copy in copies:
        copy.wait()


def fused_body(tokens, cotangent, secondary, master, m_code, v_code, m_scale, v_scale):
    f32, bf16 = jnp.float32, jnp.bfloat16
    rows, head = master.shape
    blocks = m_scale.shape[0]
    chunk = (rows, head)
    limit = 0.25 * math.sqrt(tokens.shape[1] * secondary.shape[1])
    vmem, dma = pltpu.VMEM, pltpu.SemaphoreType.DMA
    shapes = (
        ((tokens.shape[0], head), bf16),
        (chunk, f32),
        (chunk, bf16),
        (chunk, bf16),
        ((1, blocks), f32),
        ((1, blocks), f32),
        (secondary.shape, bf16),
    )
    work = 4 * tokens.shape[0] * tokens.shape[1] * head
    outs = pl.pallas_call(
        functools.partial(step_kernel, limit),
        out_shape=[vmem(shape, dtype) for shape, dtype in shapes],
        in_specs=[pl.BlockSpec(memory_space=pltpu.HBM)] * 8,
        out_specs=[pl.BlockSpec(memory_space=vmem)] * 7,
        scratch_shapes=[
            vmem(tokens.shape, bf16),
            vmem(cotangent.shape, bf16),
            vmem(secondary.shape, bf16),
            vmem(chunk, f32),
            vmem(chunk, bf16),
            vmem(chunk, bf16),
            vmem((1, blocks), f32),
            vmem((1, blocks), f32),
            vmem((4, 2, 4) + chunk, bf16),
            vmem((4, 4) + chunk, bf16),
            vmem((2, 4) + chunk, bf16),
            vmem((2, 4) + chunk, bf16),
            vmem((4,) + chunk, bf16),
            vmem((4,) + chunk, bf16),
            vmem(chunk, f32),
            vmem((3,) + chunk, bf16),
            vmem((3,) + chunk, bf16),
            vmem((4, 2, secondary.shape[0] // 2, head), bf16),
            vmem((3, 8, head), f32),
            vmem((7, 8, head), f32),
            vmem((2, 8, head), f32),
            vmem(chunk, f32),
            vmem(chunk, f32),
            dma((23,)),
            dma((2, 4)),
            dma((2, 8)),
            dma((2, 4)),
            dma((2, 3)),
            dma((2, 6)),
            dma((2, 3)),
            dma((2, 3)),
            dma((2, 7)),
            dma((2, 3)),
            dma((2, 4)),
        ],
        compiler_params=pltpu.CompilerParams(
            collective_id=0, has_side_effects=True, vmem_limit_bytes=VMEM_BYTES
        ),
        cost_estimate=pl.CostEstimate(flops=work, bytes_accessed=8 << 20, transcendentals=0),
    )(
        tokens, cotangent, secondary, master, m_code, v_code,
        m_scale.reshape(1, blocks), v_scale.reshape(1, blocks),
    )
    outs = pl.pallas_call(
        write_kernel,
        out_shape=[jax.ShapeDtypeStruct(shape, dtype) for shape, dtype in shapes],
        in_specs=[pl.BlockSpec(memory_space=vmem)] * 7,
        out_specs=[pl.BlockSpec(memory_space=pltpu.HBM)] * 7,
        scratch_shapes=[dma((7,))],
        compiler_params=pltpu.CompilerParams(vmem_limit_bytes=4 << 20),
    )(*outs)
    return (*outs[:4], outs[4].reshape(blocks), outs[5].reshape(blocks), outs[6])


def fits(mesh):
    return mesh.shape["outer"] == 8 and mesh.shape["inner"] == 4


def solution(mesh):
    in_specs = (
        P(("outer", "inner"), None),
        P(("outer", "inner"), None),
        P("inner", None),
        P(("inner", "outer"), None),
        P(("inner", "outer"), None),
        P(("inner", "outer"), None),
        P(("inner", "outer")),
        P(("inner", "outer")),
    )
    out_specs = (
        P(("outer", "inner"), None),
        P(("inner", "outer"), None),
        P(("inner", "outer"), None),
        P(("inner", "outer"), None),
        P(("inner", "outer")),
        P(("inner", "outer")),
        P("inner", None),
    )
    program = fused_body if fits(mesh) else body
    return jax.shard_map(
        program, mesh=mesh, in_specs=in_specs, out_specs=out_specs, check_vma=False
    )
```

```python
import functools
import math

import jax
import jax.numpy as jnp
from jax import lax
from jax.experimental import pallas as pl
from jax.experimental.pallas import tpu as pltpu
from jax.sharding import PartitionSpec as P

MESH = pl.DeviceIdType.MESH
PIECE = 128
VMEM_BYTES = 60 * 1024 * 1024
STEPS = (2, 1, 3, 0)


def adam_update(gradient, factor, master, m_code, v_code, m_scale, v_scale):
    blocks = m_scale.shape[0]
    height = master.shape[0] // blocks
    shaped = (blocks, height, master.shape[1])
    m_old = (m_code.astype(jnp.float32).reshape(shaped) * m_scale[:, None, None]).reshape(
        master.shape
    )
    v_old = (v_code.astype(jnp.float32).reshape(shaped) * v_scale[:, None, None]).reshape(
        master.shape
    )
    scaled = factor * gradient
    moment = 0.9 * m_old + 0.1 * scaled
    second = 0.95 * v_old + 0.05 * scaled * scaled
    master_new = master - 0.01 * (moment / (jnp.sqrt(second) + 1e-08) + 0.1 * master)
    moment_blocks = moment.reshape(blocks, -1)
    second_blocks = second.reshape(blocks, -1)
    m_scale_new = jnp.max(jnp.abs(moment_blocks), axis=1) + 1e-06
    v_scale_new = jnp.max(second_blocks, axis=1) + 1e-06
    m_code_new = (moment_blocks / m_scale_new[:, None]).reshape(master.shape).astype(jnp.bfloat16)
    v_code_new = (second_blocks / v_scale_new[:, None]).reshape(master.shape).astype(jnp.bfloat16)
    return (master_new, m_code_new, v_code_new, m_scale_new, v_scale_new)


def rounded_term(columns, cotangent):
    part = lax.dot_general(
        columns, cotangent, (((0,), (0,)), ((), ())), preferred_element_type=jnp.float32
    )
    part = lax.optimization_barrier(part.astype(jnp.bfloat16))
    return part.astype(jnp.float32)


def body(tokens, cotangent, secondary, master, m_code, v_code, m_scale, v_scale):
    tok_rows = tokens.shape[0]
    width = tokens.shape[1]
    n_outer = lax.axis_size("outer")
    n_inner = lax.axis_size("inner")
    columns = tokens
    projected = jnp.dot(
        columns,
        lax.all_gather(secondary, "inner", axis=0, tiled=True),
        preferred_element_type=jnp.float32,
    ).astype(jnp.bfloat16)
    reordered = (
        tokens.reshape(tok_rows, n_inner, n_outer, -1)
        .transpose(0, 2, 1, 3)
        .reshape(tok_rows, width)
    )
    columns = reordered
    gradient = lax.psum_scatter(
        rounded_term(columns, cotangent), ("outer", "inner"), scatter_dimension=0, tiled=True
    )
    total = lax.psum(jnp.sum(gradient * gradient), ("outer", "inner"))
    limit = 0.25 * math.sqrt(width * secondary.shape[1])
    factor = limit / jnp.maximum(jnp.sqrt(total), limit)
    master_new, m_code_new, v_code_new, m_scale_new, v_scale_new = adam_update(
        gradient, factor, master, m_code, v_code, m_scale, v_scale
    )
    secondary_new = lax.all_gather(master_new.astype(jnp.bfloat16), "outer", axis=0, tiled=True)
    return (projected, master_new, m_code_new, v_code_new, m_scale_new, v_scale_new, secondary_new)


def step_kernel(
    limit,
    tok_in, cot_in, sec_in, master_in, m_code_in, v_code_in, m_scale_in, v_scale_in,
    projected, master_new, m_code_new, v_code_new, m_scale_new, v_scale_new, sec_new,
    tok, cot, sec, master, m_code, v_code, m_scale, v_scale,
    send_a, recv_a, send_1, recv_1, send_2, recv_2, sum_3, send_3, recv_3,
    weights, sq_1, sq_2, sq_send, moments, seconds,
    sem_in, sem_a, sem_1, sem_2, sem_3, sem_w, sem_f, sem_q1, sem_q2, sem_g, sem_h, sem_p, sem_r,
):
    f32, bf16 = jnp.float32, jnp.bfloat16
    o, i = lax.axis_index("outer"), lax.axis_index("inner")
    n_z = 4
    core, z = o % 2, o // 2
    x, y = i % 2, i // 2
    to_x, to_y = i + 1 - 2 * x, i + 2 - 4 * y
    first = to_x * (1 - core) + to_y * core
    second = to_x * core + to_y * (1 - core)
    across = 3 - i
    mate = o + 1 - 2 * core
    rows = master.shape[0]
    half = sec.shape[0] // 2
    span = sec.shape[0]

    barrier = pltpu.get_barrier_semaphore()
    near = [(o, first), (o, second), (o, across)]
    far = [((o + d) % 8, i) for d in range(1, 8)]
    for peer in near + far:
        pl.semaphore_signal(barrier, inc=1, device_id=peer, device_id_type=MESH)

    loads = []

    def load(src, dst):
        loads.append(pltpu.make_async_copy(src, dst, sem_in.at[len(loads)]))
        loads[-1].start()

    load(cot_in, cot)
    groups = (across, second, first, i)
    pair = 2 * rows

    def columns_of(g, s):
        start = groups[g] * span + ((z + STEPS[s]) % n_z) * pair
        return pl.multiple_of(start, 128)

    for s in range(4):
        for g in range(4):
            columns = pl.ds(columns_of(g, s), pair)
            load(tok_in.at[:, columns], tok.at[:, columns])
        if s == 0:
            load(sec_in, sec)
    load(master_in, master)
    load(m_code_in, m_code)
    load(v_code_in, v_code)
    load(m_scale_in, m_scale)
    load(v_scale_in, v_scale)

    started = []

    def send(src, dst, sems, index, peer):
        copy = pltpu.make_async_remote_copy(
            src_ref=src, dst_ref=dst,
            send_sem=sems.at[0, index], recv_sem=sems.at[1, index],
            device_id=peer, device_id_type=MESH,
        )
        copy.start()
        started.append(copy)
        return copy

    def arrived(dst, sems, index):
        pltpu.make_async_remote_copy(
            src_ref=dst, dst_ref=dst,
            send_sem=sems.at[0, index], recv_sem=sems.at[1, index],
            device_id=(mate, i), device_id_type=MESH,
        ).wait_recv()

    def weight_part(j, part):
        third = half // 3
        return weights.at[j, core, pl.ds(part * third, third + part * third)]

    def send_weights(part):
        third = half // 3
        start = pl.multiple_of(core * half + part * third, 128)
        source = sec.at[pl.ds(start, third + part * third)]
        for index, peer in enumerate((first, second)):
            send(source, weight_part(i, part), sem_w, 2 * part + index, (o, peer))

    def partials(s, c):
        for g in range(4):
            start = pl.multiple_of(columns_of(g, s) + c * rows, 128)
            part = lax.dot_general(
                tok[:, pl.ds(start, rows)], cot[...], (((0,), (0,)), ((), ())),
                preferred_element_type=f32,
            )
            send_a[s, c, g] = part.astype(bf16)

    def for_both(s):
        for g in range(4):
            loads[1 + 4 * s + g + (s > 0)].wait()
        partials(s, 1 - core)
        if s == 0:
            pl.semaphore_wait(barrier, 10)
        send(send_a.at[s, 1 - core], recv_a.at[s], sem_a, s, (mate, i))
        partials(s, core)

    def chip_sum(q, s):
        own = send_a[s, core, (0, 2, 1, 3)[q]]
        return own.astype(f32) + recv_a[s, q].astype(f32)

    def to_first(s):
        arrived(recv_a.at[s], sem_a, s)
        for q in range(2):
            send_1[q, s] = chip_sum(q, s).astype(bf16)
            send(send_1.at[q, s], recv_1.at[q, s], sem_1, q * 4 + s, (o, first))

    def to_second(s):
        arrived(recv_1.at[0, s], sem_1, s)
        send_2[s] = (chip_sum(2, s) + recv_1[0, s].astype(f32)).astype(bf16)
        send(send_2.at[s], recv_2.at[s], sem_2, s, (o, second))

    def along_z(s):
        arrived(recv_1.at[1, s], sem_1, 4 + s)
        arrived(recv_2.at[s], sem_2, s)
        total = chip_sum(3, s) + recv_1[1, s].astype(f32) + recv_2[s].astype(f32)
        if STEPS[s]:
            d = STEPS[s]
            send_3[d - 1] = total.astype(bf16)
            peer = ((z + d) % n_z) * 2 + core
            send(send_3.at[d - 1], recv_3.at[d - 1], sem_3, d - 1, (peer, i))
        else:
            sum_3[...] = total

    loads[0].wait()
    for_both(0)
    loads[5].wait()
    send_weights(0)
    for_both(1)
    to_first(0)
    for_both(2)
    to_first(1)
    for_both(3)
    to_second(0)
    to_first(2)
    to_second(1)
    to_first(3)
    along_z(0)
    to_second(2)
    along_z(1)
    to_second(3)
    along_z(2)
    along_z(3)

    send_weights(1)
    arrived(weight_part(first, 0), sem_w, 0)
    send(weight_part(first, 0), weight_part(first, 0), sem_w, 4, (o, second))
    arrived(weight_part(second, 0), sem_w, 1)

    own_columns = tok[:, pl.ds(pl.multiple_of(i * span, 128), span)]
    out = jnp.dot(own_columns, sec[...], preferred_element_type=f32)

    for d in (1, 3, 2):
        arrived(recv_3.at[d - 1], sem_3, d - 1)
    gradient = sum_3[...]
    for d in range(1, 4):
        gradient = gradient + recv_3[d - 1].astype(f32)
    sum_3[...] = gradient

    squares = jnp.sum((gradient * gradient).reshape(rows // 8, 8, 128), axis=0)
    sq_send[0] = squares
    for d in range(1, 8):
        send(sq_send.at[0], sq_2.at[d - 1], sem_q2, d - 1, ((o + d) % 8, i))
    for copy in loads[18:]:
        copy.wait()
    height = rows // m_scale.shape[1]

    def block_mask(p):
        shape = (PIECE, m_scale.shape[1])
        row = lax.broadcasted_iota(jnp.int32, shape, 0) + p * PIECE
        return row // height == lax.broadcasted_iota(jnp.int32, shape, 1)

    def expand(p, scales):
        return jnp.sum(jnp.where(block_mask(p), scales, 0.0), axis=1, keepdims=True)

    pieces = rows // PIECE
    for p in range(pieces):
        part = pl.ds(p * PIECE, PIECE)
        moments[part, :] = 0.9 * (m_code[part, :].astype(f32) * expand(p, m_scale[...]))
        seconds[part, :] = 0.95 * (v_code[part, :].astype(f32) * expand(p, v_scale[...]))

    for d in range(1, 8):
        arrived(sq_2.at[d - 1], sem_q2, d - 1)
        squares = squares + sq_2[d - 1]
    sq_send[1] = squares
    for index, peer in enumerate((first, second, across)):
        send(sq_send.at[1], sq_1.at[index], sem_q1, index, (o, peer))
    for index in range(3):
        arrived(sq_1.at[index], sem_q1, index)
        squares = squares + sq_1[index]
    square_sum = jnp.sum(jnp.sum(squares, axis=0, keepdims=True), axis=1, keepdims=True)
    factor = limit / jnp.maximum(jnp.sqrt(square_sum), limit)

    def new_rows(owner):
        return sec_new.at[pl.ds(pl.multiple_of(owner * rows, 128), rows)]

    def new_piece(owner, p):
        return sec_new.at[pl.ds(pl.multiple_of(owner * rows + p * PIECE, 128), PIECE)]

    for p in range(pieces):
        part = pl.ds(p * PIECE, PIECE)
        scaled = factor * sum_3[part, :]
        moment = moments[part, :] + 0.1 * scaled
        second_new = seconds[part, :] + 0.05 * scaled * scaled
        old = master[part, :]
        new = old - 0.01 * (moment / (jnp.sqrt(second_new) + 1e-08) + 0.1 * old)
        moments[part, :] = moment
        seconds[part, :] = second_new
        master_new[part, :] = new
        sec_new[pl.ds(pl.multiple_of(o * rows + p * PIECE, 128), PIECE), :] = new.astype(bf16)
        send(new_piece(o, p), new_piece(o, p), sem_p, p, (((z + 2) % n_z) * 2 + core, i))

    def neighbour(d):
        peer = (((z + d) % n_z) * 2 + core, i)
        return pltpu.make_async_remote_copy(
            src_ref=new_rows(o), dst_ref=new_rows(o),
            send_sem=sem_g.at[0, d - 1], recv_sem=sem_g.at[1, d - 1],
            device_id=peer, device_id_type=MESH,
        )

    guarded = [(z < n_z - 1, neighbour(1)), (z > 0, neighbour(3))]
    for needed, copy in guarded:
        pl.when(needed)(copy.start)
    send(new_rows(o), new_rows(o), sem_h, 0, (mate, i))

    arrived(weight_part(first, 1), sem_w, 2)
    send(weight_part(first, 1), weight_part(first, 1), sem_w, 5, (o, second))
    send(weights.at[first, core], weights.at[first, core], sem_f, 0, (mate, i))
    arrived(weight_part(second, 1), sem_w, 3)
    send(weights.at[second, core], weights.at[second, core], sem_f, 1, (mate, i))

    m_row = jnp.zeros(m_scale.shape, f32)
    v_row = jnp.zeros(v_scale.shape, f32)
    for p in range(pieces):
        part = pl.ds(p * PIECE, PIECE)
        mask = block_mask(p)
        for values, codes, is_m in ((moments, m_code_new, True), (seconds, v_code_new, False)):
            value = values[part, :]
            tops = jnp.max(jnp.abs(value), axis=1, keepdims=True)
            top = jnp.max(jnp.where(mask, tops, 0.0), axis=0, keepdims=True)
            scale = top + 1e-06
            codes[part, :] = (value / expand(p, scale)).astype(bf16)
            if is_m:
                m_row = jnp.maximum(m_row, top)
            else:
                v_row = jnp.maximum(v_row, top)
    m_scale_new[...] = m_row + 1e-06
    v_scale_new[...] = v_row + 1e-06

    def product(j, h):
        start = pl.multiple_of(j * span + h * half, 128)
        return jnp.dot(tok[:, pl.ds(start, half)], weights[j, h], preferred_element_type=f32)

    def gathered(d):
        owner = ((z + n_z - d) % n_z) * 2 + core
        if d != 2:
            arrived(new_rows(owner), sem_g, d - 1)
        else:
            for p in range(pieces):
                arrived(new_piece(owner, p), sem_p, p)
            inside = (z > 0) & (z < n_z - 1)
            index = (2 * z + 2) % n_z
            end = (z // 2) * (n_z - 1)
            copy = pltpu.make_async_remote_copy(
                src_ref=new_rows(owner), dst_ref=new_rows(owner),
                send_sem=sem_r.at[0], recv_sem=sem_g.at[1, index],
                device_id=(end * 2 + core, i), device_id_type=MESH,
            )
            pl.when(inside)(copy.start)
            guarded.append((inside, copy))
        send(new_rows(owner), new_rows(owner), sem_h, d, (mate, i))

    out = out + product(first, core)
    out = out + product(second, core)
    gathered(2)
    arrived(weight_part(across, 0), sem_w, 4)
    arrived(weight_part(across, 1), sem_w, 5)
    send(weights.at[across, core], weights.at[across, core], sem_f, 2, (mate, i))
    out = out + product(across, core)
    for index, j in enumerate((second, first)):
        arrived(weights.at[j, 1 - core], sem_f, index)
        out = out + product(j, 1 - core)
    gathered(1)
    gathered(3)
    arrived(weights.at[across, 1 - core], sem_f, 2)
    out = out + product(across, 1 - core)
    projected[...] = out.astype(bf16)
    for d in range(4):
        owner = ((z + n_z - d) % n_z) * 2 + 1 - core
        arrived(new_rows(owner), sem_h, d)
    for copy in started:
        copy.wait_send()
    for needed, copy in guarded:
        pl.when(needed)(copy.wait_send)


def write_kernel(*refs):
    count = len(refs) // 2
    sems = refs[-1]
    copies = [
        pltpu.make_async_copy(refs[k], refs[count + k], sems.at[k]) for k in range(count)
    ]
    for copy in copies:
        copy.start()
    for copy in copies:
        copy.wait()


def fused_body(tokens, cotangent, secondary, master, m_code, v_code, m_scale, v_scale):
    f32, bf16 = jnp.float32, jnp.bfloat16
    rows, head = master.shape
    blocks = m_scale.shape[0]
    chunk = (rows, head)
    limit = 0.25 * math.sqrt(tokens.shape[1] * secondary.shape[1])
    vmem, dma = pltpu.VMEM, pltpu.SemaphoreType.DMA
    shapes = (
        ((tokens.shape[0], head), bf16),
        (chunk, f32),
        (chunk, bf16),
        (chunk, bf16),
        ((1, blocks), f32),
        ((1, blocks), f32),
        (secondary.shape, bf16),
    )
    work = 4 * tokens.shape[0] * tokens.shape[1] * head
    outs = pl.pallas_call(
        functools.partial(step_kernel, limit),
        out_shape=[vmem(shape, dtype) for shape, dtype in shapes],
        in_specs=[pl.BlockSpec(memory_space=pltpu.HBM)] * 8,
        out_specs=[pl.BlockSpec(memory_space=vmem)] * 7,
        scratch_shapes=[
            vmem(tokens.shape, bf16),
            vmem(cotangent.shape, bf16),
            vmem(secondary.shape, bf16),
            vmem(chunk, f32),
            vmem(chunk, bf16),
            vmem(chunk, bf16),
            vmem((1, blocks), f32),
            vmem((1, blocks), f32),
            vmem((4, 2, 4) + chunk, bf16),
            vmem((4, 4) + chunk, bf16),
            vmem((2, 4) + chunk, bf16),
            vmem((2, 4) + chunk, bf16),
            vmem((4,) + chunk, bf16),
            vmem((4,) + chunk, bf16),
            vmem(chunk, f32),
            vmem((3,) + chunk, bf16),
            vmem((3,) + chunk, bf16),
            vmem((4, 2, secondary.shape[0] // 2, head), bf16),
            vmem((3, 8, head), f32),
            vmem((7, 8, head), f32),
            vmem((2, 8, head), f32),
            vmem(chunk, f32),
            vmem(chunk, f32),
            dma((23,)),
            dma((2, 4)),
            dma((2, 8)),
            dma((2, 4)),
            dma((2, 3)),
            dma((2, 6)),
            dma((2, 3)),
            dma((2, 3)),
            dma((2, 7)),
            dma((2, 3)),
            dma((2, 4)),
            dma((2, 3)),
            dma((1,)),
        ],
        compiler_params=pltpu.CompilerParams(
            collective_id=0, has_side_effects=True, vmem_limit_bytes=VMEM_BYTES
        ),
        cost_estimate=pl.CostEstimate(flops=work, bytes_accessed=8 << 20, transcendentals=0),
    )(
        tokens, cotangent, secondary, master, m_code, v_code,
        m_scale.reshape(1, blocks), v_scale.reshape(1, blocks),
    )
    outs = pl.pallas_call(
        write_kernel,
        out_shape=[jax.ShapeDtypeStruct(shape, dtype) for shape, dtype in shapes],
        in_specs=[pl.BlockSpec(memory_space=vmem)] * 7,
        out_specs=[pl.BlockSpec(memory_space=pltpu.HBM)] * 7,
        scratch_shapes=[dma((7,))],
        compiler_params=pltpu.CompilerParams(vmem_limit_bytes=4 << 20),
    )(*outs)
    return (*outs[:4], outs[4].reshape(blocks), outs[5].reshape(blocks), outs[6])


def fits(mesh):
    return mesh.shape["outer"] == 8 and mesh.shape["inner"] == 4


def solution(mesh):
    in_specs = (
        P(("outer", "inner"), None),
        P(("outer", "inner"), None),
        P("inner", None),
        P(("inner", "outer"), None),
        P(("inner", "outer"), None),
        P(("inner", "outer"), None),
        P(("inner", "outer")),
        P(("inner", "outer")),
    )
    out_specs = (
        P(("outer", "inner"), None),
        P(("inner", "outer"), None),
        P(("inner", "outer"), None),
        P(("inner", "outer"), None),
        P(("inner", "outer")),
        P(("inner", "outer")),
        P("inner", None),
    )
    program = fused_body if fits(mesh) else body
    return jax.shard_map(
        program, mesh=mesh, in_specs=in_specs, out_specs=out_specs, check_vma=False
    )
```

```python
import functools
import math

import jax
import jax.numpy as jnp
from jax import lax
from jax.experimental import pallas as pl
from jax.experimental.pallas import tpu as pltpu
from jax.sharding import PartitionSpec as P

MESH = pl.DeviceIdType.MESH
PIECE = 128
VMEM_BYTES = 60 * 1024 * 1024
STEPS = (2, 1, 3, 0)


def adam_update(gradient, factor, master, m_code, v_code, m_scale, v_scale):
    blocks = m_scale.shape[0]
    height = master.shape[0] // blocks
    shaped = (blocks, height, master.shape[1])
    m_old = (m_code.astype(jnp.float32).reshape(shaped) * m_scale[:, None, None]).reshape(
        master.shape
    )
    v_old = (v_code.astype(jnp.float32).reshape(shaped) * v_scale[:, None, None]).reshape(
        master.shape
    )
    scaled = factor * gradient
    moment = 0.9 * m_old + 0.1 * scaled
    second = 0.95 * v_old + 0.05 * scaled * scaled
    master_new = master - 0.01 * (moment / (jnp.sqrt(second) + 1e-08) + 0.1 * master)
    moment_blocks = moment.reshape(blocks, -1)
    second_blocks = second.reshape(blocks, -1)
    m_scale_new = jnp.max(jnp.abs(moment_blocks), axis=1) + 1e-06
    v_scale_new = jnp.max(second_blocks, axis=1) + 1e-06
    m_code_new = (moment_blocks / m_scale_new[:, None]).reshape(master.shape).astype(jnp.bfloat16)
    v_code_new = (second_blocks / v_scale_new[:, None]).reshape(master.shape).astype(jnp.bfloat16)
    return (master_new, m_code_new, v_code_new, m_scale_new, v_scale_new)


def rounded_term(columns, cotangent):
    part = lax.dot_general(
        columns, cotangent, (((0,), (0,)), ((), ())), preferred_element_type=jnp.float32
    )
    part = lax.optimization_barrier(part.astype(jnp.bfloat16))
    return part.astype(jnp.float32)


def body(tokens, cotangent, secondary, master, m_code, v_code, m_scale, v_scale):
    tok_rows = tokens.shape[0]
    width = tokens.shape[1]
    n_outer = lax.axis_size("outer")
    n_inner = lax.axis_size("inner")
    columns = tokens
    projected = jnp.dot(
        columns,
        lax.all_gather(secondary, "inner", axis=0, tiled=True),
        preferred_element_type=jnp.float32,
    ).astype(jnp.bfloat16)
    reordered = (
        tokens.reshape(tok_rows, n_inner, n_outer, -1)
        .transpose(0, 2, 1, 3)
        .reshape(tok_rows, width)
    )
    columns = reordered
    gradient = lax.psum_scatter(
        rounded_term(columns, cotangent), ("outer", "inner"), scatter_dimension=0, tiled=True
    )
    total = lax.psum(jnp.sum(gradient * gradient), ("outer", "inner"))
    limit = 0.25 * math.sqrt(width * secondary.shape[1])
    factor = limit / jnp.maximum(jnp.sqrt(total), limit)
    master_new, m_code_new, v_code_new, m_scale_new, v_scale_new = adam_update(
        gradient, factor, master, m_code, v_code, m_scale, v_scale
    )
    secondary_new = lax.all_gather(master_new.astype(jnp.bfloat16), "outer", axis=0, tiled=True)
    return (projected, master_new, m_code_new, v_code_new, m_scale_new, v_scale_new, secondary_new)


def step_kernel(
    limit,
    tok_in, cot_in, sec_in, master_in, m_code_in, v_code_in, m_scale_in, v_scale_in,
    projected, master_new, m_code_new, v_code_new, m_scale_new, v_scale_new, sec_new,
    tok, cot, sec, master, m_code, v_code, m_scale, v_scale,
    send_a, recv_a, send_1, recv_1, send_2, recv_2, sum_3, send_3, recv_3,
    weights, sq_1, sq_2, sq_send, moments, seconds,
    sem_in, sem_a, sem_1, sem_2, sem_3, sem_w, sem_f, sem_q1, sem_q2, sem_g, sem_h, sem_p, sem_r,
):
    f32, bf16 = jnp.float32, jnp.bfloat16
    o, i = lax.axis_index("outer"), lax.axis_index("inner")
    n_z = 4
    core, z = o % 2, o // 2
    x, y = i % 2, i // 2
    to_x, to_y = i + 1 - 2 * x, i + 2 - 4 * y
    first = to_x * (1 - core) + to_y * core
    second = to_x * core + to_y * (1 - core)
    across = 3 - i
    mate = o + 1 - 2 * core
    rows = master.shape[0]
    half = sec.shape[0] // 2
    span = sec.shape[0]

    barrier = pltpu.get_barrier_semaphore()
    near = [(o, first), (o, second), (o, across)]
    far = [((o + d) % 8, i) for d in range(1, 8)]
    for peer in near + far:
        pl.semaphore_signal(barrier, inc=1, device_id=peer, device_id_type=MESH)

    loads = []

    def load(src, dst):
        loads.append(pltpu.make_async_copy(src, dst, sem_in.at[len(loads)]))
        loads[-1].start()

    load(cot_in, cot)
    groups = (across, second, first, i)
    pair = 2 * rows

    def columns_of(g, s):
        start = groups[g] * span + ((z + STEPS[s]) % n_z) * pair
        return pl.multiple_of(start, 128)

    for s in range(4):
        for g in range(4):
            columns = pl.ds(columns_of(g, s), pair)
            load(tok_in.at[:, columns], tok.at[:, columns])
        if s == 0:
            load(sec_in, sec)
    load(master_in, master)
    load(m_code_in, m_code)
    load(v_code_in, v_code)
    load(m_scale_in, m_scale)
    load(v_scale_in, v_scale)

    started = []

    def send(src, dst, sems, index, peer):
        copy = pltpu.make_async_remote_copy(
            src_ref=src, dst_ref=dst,
            send_sem=sems.at[0, index], recv_sem=sems.at[1, index],
            device_id=peer, device_id_type=MESH,
        )
        copy.start()
        started.append(copy)
        return copy

    def arrived(dst, sems, index):
        pltpu.make_async_remote_copy(
            src_ref=dst, dst_ref=dst,
            send_sem=sems.at[0, index], recv_sem=sems.at[1, index],
            device_id=(mate, i), device_id_type=MESH,
        ).wait_recv()

    def weight_part(j, part):
        third = half // 3
        return weights.at[j, core, pl.ds(part * third, third + part * third)]

    def send_weights(part):
        third = half // 3
        start = pl.multiple_of(core * half + part * third, 128)
        source = sec.at[pl.ds(start, third + part * third)]
        for index, peer in enumerate((first, second)):
            send(source, weight_part(i, part), sem_w, 2 * part + index, (o, peer))

    def partials(s, c):
        for g in range(4):
            start = pl.multiple_of(columns_of(g, s) + c * rows, 128)
            part = lax.dot_general(
                tok[:, pl.ds(start, rows)], cot[...], (((0,), (0,)), ((), ())),
                preferred_element_type=f32,
            )
            send_a[s, c, g] = part.astype(bf16)

    def for_both(s):
        for g in range(4):
            loads[1 + 4 * s + g + (s > 0)].wait()
        partials(s, 1 - core)
        if s == 0:
            pl.semaphore_wait(barrier, 10)
        send(send_a.at[s, 1 - core], recv_a.at[s], sem_a, s, (mate, i))
        partials(s, core)

    def chip_sum(q, s):
        own = send_a[s, core, (0, 2, 1, 3)[q]]
        return own.astype(f32) + recv_a[s, q].astype(f32)

    def to_first(s):
        arrived(recv_a.at[s], sem_a, s)
        for q in range(2):
            send_1[q, s] = chip_sum(q, s).astype(bf16)
            send(send_1.at[q, s], recv_1.at[q, s], sem_1, q * 4 + s, (o, first))

    def to_second(s):
        arrived(recv_1.at[0, s], sem_1, s)
        send_2[s] = (chip_sum(2, s) + recv_1[0, s].astype(f32)).astype(bf16)
        send(send_2.at[s], recv_2.at[s], sem_2, s, (o, second))

    def along_z(s):
        arrived(recv_1.at[1, s], sem_1, 4 + s)
        arrived(recv_2.at[s], sem_2, s)
        total = chip_sum(3, s) + recv_1[1, s].astype(f32) + recv_2[s].astype(f32)
        if STEPS[s]:
            d = STEPS[s]
            send_3[d - 1] = total.astype(bf16)
            peer = ((z + d) % n_z) * 2 + core
            send(send_3.at[d - 1], recv_3.at[d - 1], sem_3, d - 1, (peer, i))
        else:
            sum_3[...] = total

    loads[0].wait()
    for_both(0)
    loads[5].wait()
    send_weights(0)
    for_both(1)
    to_first(0)
    for_both(2)
    to_first(1)
    for_both(3)
    to_second(0)
    to_first(2)
    to_second(1)
    to_first(3)
    along_z(0)
    to_second(2)
    along_z(1)
    to_second(3)
    along_z(2)
    along_z(3)

    send_weights(1)
    arrived(weight_part(first, 0), sem_w, 0)
    send(weight_part(first, 0), weight_part(first, 0), sem_w, 4, (o, second))
    arrived(weight_part(second, 0), sem_w, 1)

    own_columns = tok[:, pl.ds(pl.multiple_of(i * span, 128), span)]
    out = jnp.dot(own_columns, sec[...], preferred_element_type=f32)

    for d in (1, 3, 2):
        arrived(recv_3.at[d - 1], sem_3, d - 1)
    gradient = sum_3[...]
    for d in range(1, 4):
        gradient = gradient + recv_3[d - 1].astype(f32)
    sum_3[...] = gradient

    squares = jnp.sum((gradient * gradient).reshape(rows // 8, 8, 128), axis=0)
    sq_send[0] = squares
    for d in range(1, 8):
        send(sq_send.at[0], sq_2.at[d - 1], sem_q2, d - 1, ((o + d) % 8, i))
    for copy in loads[18:]:
        copy.wait()
    height = rows // m_scale.shape[1]

    def block_mask(p):
        shape = (PIECE, m_scale.shape[1])
        row = lax.broadcasted_iota(jnp.int32, shape, 0) + p * PIECE
        return row // height == lax.broadcasted_iota(jnp.int32, shape, 1)

    def expand(p, scales):
        return jnp.sum(jnp.where(block_mask(p), scales, 0.0), axis=1, keepdims=True)

    pieces = rows // PIECE
    for p in range(pieces):
        part = pl.ds(p * PIECE, PIECE)
        moments[part, :] = 0.9 * (m_code[part, :].astype(f32) * expand(p, m_scale[...]))
        seconds[part, :] = 0.95 * (v_code[part, :].astype(f32) * expand(p, v_scale[...]))

    for d in range(1, 8):
        arrived(sq_2.at[d - 1], sem_q2, d - 1)
        squares = squares + sq_2[d - 1]
    sq_send[1] = squares
    for index, peer in enumerate((first, second, across)):
        send(sq_send.at[1], sq_1.at[index], sem_q1, index, (o, peer))
    arrived(weight_part(first, 1), sem_w, 2)
    send(weight_part(first, 1), weight_part(first, 1), sem_w, 5, (o, second))
    send(weights.at[first, core], weights.at[first, core], sem_f, 0, (mate, i))
    arrived(weight_part(second, 1), sem_w, 3)
    send(weights.at[second, core], weights.at[second, core], sem_f, 1, (mate, i))

    for index in range(3):
        arrived(sq_1.at[index], sem_q1, index)
        squares = squares + sq_1[index]
    square_sum = jnp.sum(jnp.sum(squares, axis=0, keepdims=True), axis=1, keepdims=True)
    factor = limit / jnp.maximum(jnp.sqrt(square_sum), limit)

    def new_rows(owner):
        return sec_new.at[pl.ds(pl.multiple_of(owner * rows, 128), rows)]

    def new_piece(owner, p):
        return sec_new.at[pl.ds(pl.multiple_of(owner * rows + p * PIECE, 128), PIECE)]

    for p in range(pieces):
        part = pl.ds(p * PIECE, PIECE)
        scaled = factor * sum_3[part, :]
        moment = moments[part, :] + 0.1 * scaled
        second_new = seconds[part, :] + 0.05 * scaled * scaled
        old = master[part, :]
        new = old - 0.01 * (moment / (jnp.sqrt(second_new) + 1e-08) + 0.1 * old)
        moments[part, :] = moment
        seconds[part, :] = second_new
        master_new[part, :] = new
        sec_new[pl.ds(pl.multiple_of(o * rows + p * PIECE, 128), PIECE), :] = new.astype(bf16)
        send(new_piece(o, p), new_piece(o, p), sem_p, p, (((z + 2) % n_z) * 2 + core, i))

    def neighbour(d):
        peer = (((z + d) % n_z) * 2 + core, i)
        return pltpu.make_async_remote_copy(
            src_ref=new_rows(o), dst_ref=new_rows(o),
            send_sem=sem_g.at[0, d - 1], recv_sem=sem_g.at[1, d - 1],
            device_id=peer, device_id_type=MESH,
        )

    guarded = [(z < n_z - 1, neighbour(1)), (z > 0, neighbour(3))]
    for needed, copy in guarded:
        pl.when(needed)(copy.start)
    send(new_rows(o), new_rows(o), sem_h, 0, (mate, i))

    m_row = jnp.zeros(m_scale.shape, f32)
    v_row = jnp.zeros(v_scale.shape, f32)
    for p in range(pieces):
        part = pl.ds(p * PIECE, PIECE)
        mask = block_mask(p)
        for values, codes, is_m in ((moments, m_code_new, True), (seconds, v_code_new, False)):
            value = values[part, :]
            tops = jnp.max(jnp.abs(value), axis=1, keepdims=True)
            top = jnp.max(jnp.where(mask, tops, 0.0), axis=0, keepdims=True)
            scale = top + 1e-06
            codes[part, :] = (value / expand(p, scale)).astype(bf16)
            if is_m:
                m_row = jnp.maximum(m_row, top)
            else:
                v_row = jnp.maximum(v_row, top)
    m_scale_new[...] = m_row + 1e-06
    v_scale_new[...] = v_row + 1e-06

    def product(j, h):
        start = pl.multiple_of(j * span + h * half, 128)
        return jnp.dot(tok[:, pl.ds(start, half)], weights[j, h], preferred_element_type=f32)

    def gathered(d):
        owner = ((z + n_z - d) % n_z) * 2 + core
        if d != 2:
            arrived(new_rows(owner), sem_g, d - 1)
        else:
            for p in range(pieces):
                arrived(new_piece(owner, p), sem_p, p)
            inside = (z > 0) & (z < n_z - 1)
            index = (2 * z + 2) % n_z
            end = (z // 2) * (n_z - 1)
            copy = pltpu.make_async_remote_copy(
                src_ref=new_rows(owner), dst_ref=new_rows(owner),
                send_sem=sem_r.at[0], recv_sem=sem_g.at[1, index],
                device_id=(end * 2 + core, i), device_id_type=MESH,
            )
            pl.when(inside)(copy.start)
            guarded.append((inside, copy))
        send(new_rows(owner), new_rows(owner), sem_h, d, (mate, i))

    out = out + product(first, core)
    out = out + product(second, core)
    gathered(2)
    arrived(weight_part(across, 0), sem_w, 4)
    arrived(weight_part(across, 1), sem_w, 5)
    send(weights.at[across, core], weights.at[across, core], sem_f, 2, (mate, i))
    out = out + product(across, core)
    for index, j in enumerate((second, first)):
        arrived(weights.at[j, 1 - core], sem_f, index)
        out = out + product(j, 1 - core)
    gathered(1)
    gathered(3)
    arrived(weights.at[across, 1 - core], sem_f, 2)
    out = out + product(across, 1 - core)
    projected[...] = out.astype(bf16)
    for d in range(4):
        owner = ((z + n_z - d) % n_z) * 2 + 1 - core
        arrived(new_rows(owner), sem_h, d)
    for copy in started:
        copy.wait_send()
    for needed, copy in guarded:
        pl.when(needed)(copy.wait_send)


def write_kernel(*refs):
    count = len(refs) // 2
    sems = refs[-1]
    copies = [
        pltpu.make_async_copy(refs[k], refs[count + k], sems.at[k]) for k in range(count)
    ]
    for copy in copies:
        copy.start()
    for copy in copies:
        copy.wait()


def fused_body(tokens, cotangent, secondary, master, m_code, v_code, m_scale, v_scale):
    f32, bf16 = jnp.float32, jnp.bfloat16
    rows, head = master.shape
    blocks = m_scale.shape[0]
    chunk = (rows, head)
    limit = 0.25 * math.sqrt(tokens.shape[1] * secondary.shape[1])
    vmem, dma = pltpu.VMEM, pltpu.SemaphoreType.DMA
    shapes = (
        ((tokens.shape[0], head), bf16),
        (chunk, f32),
        (chunk, bf16),
        (chunk, bf16),
        ((1, blocks), f32),
        ((1, blocks), f32),
        (secondary.shape, bf16),
    )
    work = 4 * tokens.shape[0] * tokens.shape[1] * head
    outs = pl.pallas_call(
        functools.partial(step_kernel, limit),
        out_shape=[vmem(shape, dtype) for shape, dtype in shapes],
        in_specs=[pl.BlockSpec(memory_space=pltpu.HBM)] * 8,
        out_specs=[pl.BlockSpec(memory_space=vmem)] * 7,
        scratch_shapes=[
            vmem(tokens.shape, bf16),
            vmem(cotangent.shape, bf16),
            vmem(secondary.shape, bf16),
            vmem(chunk, f32),
            vmem(chunk, bf16),
            vmem(chunk, bf16),
            vmem((1, blocks), f32),
            vmem((1, blocks), f32),
            vmem((4, 2, 4) + chunk, bf16),
            vmem((4, 4) + chunk, bf16),
            vmem((2, 4) + chunk, bf16),
            vmem((2, 4) + chunk, bf16),
            vmem((4,) + chunk, bf16),
            vmem((4,) + chunk, bf16),
            vmem(chunk, f32),
            vmem((3,) + chunk, bf16),
            vmem((3,) + chunk, bf16),
            vmem((4, 2, secondary.shape[0] // 2, head), bf16),
            vmem((3, 8, head), f32),
            vmem((7, 8, head), f32),
            vmem((2, 8, head), f32),
            vmem(chunk, f32),
            vmem(chunk, f32),
            dma((23,)),
            dma((2, 4)),
            dma((2, 8)),
            dma((2, 4)),
            dma((2, 3)),
            dma((2, 6)),
            dma((2, 3)),
            dma((2, 3)),
            dma((2, 7)),
            dma((2, 3)),
            dma((2, 4)),
            dma((2, 3)),
            dma((1,)),
        ],
        compiler_params=pltpu.CompilerParams(
            collective_id=0, has_side_effects=True, vmem_limit_bytes=VMEM_BYTES
        ),
        cost_estimate=pl.CostEstimate(flops=work, bytes_accessed=8 << 20, transcendentals=0),
    )(
        tokens, cotangent, secondary, master, m_code, v_code,
        m_scale.reshape(1, blocks), v_scale.reshape(1, blocks),
    )
    outs = pl.pallas_call(
        write_kernel,
        out_shape=[jax.ShapeDtypeStruct(shape, dtype) for shape, dtype in shapes],
        in_specs=[pl.BlockSpec(memory_space=vmem)] * 7,
        out_specs=[pl.BlockSpec(memory_space=pltpu.HBM)] * 7,
        scratch_shapes=[dma((7,))],
        compiler_params=pltpu.CompilerParams(vmem_limit_bytes=4 << 20),
    )(*outs)
    return (*outs[:4], outs[4].reshape(blocks), outs[5].reshape(blocks), outs[6])


def fits(mesh):
    return mesh.shape["outer"] == 8 and mesh.shape["inner"] == 4


def solution(mesh):
    in_specs = (
        P(("outer", "inner"), None),
        P(("outer", "inner"), None),
        P("inner", None),
        P(("inner", "outer"), None),
        P(("inner", "outer"), None),
        P(("inner", "outer"), None),
        P(("inner", "outer")),
        P(("inner", "outer")),
    )
    out_specs = (
        P(("outer", "inner"), None),
        P(("inner", "outer"), None),
        P(("inner", "outer"), None),
        P(("inner", "outer"), None),
        P(("inner", "outer")),
        P(("inner", "outer")),
        P("inner", None),
    )
    program = fused_body if fits(mesh) else body
    return jax.shard_map(
        program, mesh=mesh, in_specs=in_specs, out_specs=out_specs, check_vma=False
    )
```

```python
import functools
import math

import jax
import jax.numpy as jnp
from jax import lax
from jax.experimental import pallas as pl
from jax.experimental.pallas import tpu as pltpu
from jax.sharding import PartitionSpec as P

MESH = pl.DeviceIdType.MESH
PIECE = 128
VMEM_BYTES = 60 * 1024 * 1024
STEPS = (2, 1, 3, 0)


def adam_update(gradient, factor, master, m_code, v_code, m_scale, v_scale):
    blocks = m_scale.shape[0]
    height = master.shape[0] // blocks
    shaped = (blocks, height, master.shape[1])
    m_old = (m_code.astype(jnp.float32).reshape(shaped) * m_scale[:, None, None]).reshape(
        master.shape
    )
    v_old = (v_code.astype(jnp.float32).reshape(shaped) * v_scale[:, None, None]).reshape(
        master.shape
    )
    scaled = factor * gradient
    moment = 0.9 * m_old + 0.1 * scaled
    second = 0.95 * v_old + 0.05 * scaled * scaled
    master_new = master - 0.01 * (moment / (jnp.sqrt(second) + 1e-08) + 0.1 * master)
    moment_blocks = moment.reshape(blocks, -1)
    second_blocks = second.reshape(blocks, -1)
    m_scale_new = jnp.max(jnp.abs(moment_blocks), axis=1) + 1e-06
    v_scale_new = jnp.max(second_blocks, axis=1) + 1e-06
    m_code_new = (moment_blocks / m_scale_new[:, None]).reshape(master.shape).astype(jnp.bfloat16)
    v_code_new = (second_blocks / v_scale_new[:, None]).reshape(master.shape).astype(jnp.bfloat16)
    return (master_new, m_code_new, v_code_new, m_scale_new, v_scale_new)


def rounded_term(columns, cotangent):
    part = lax.dot_general(
        columns, cotangent, (((0,), (0,)), ((), ())), preferred_element_type=jnp.float32
    )
    part = lax.optimization_barrier(part.astype(jnp.bfloat16))
    return part.astype(jnp.float32)


def body(tokens, cotangent, secondary, master, m_code, v_code, m_scale, v_scale):
    tok_rows = tokens.shape[0]
    width = tokens.shape[1]
    n_outer = lax.axis_size("outer")
    n_inner = lax.axis_size("inner")
    columns = tokens
    projected = jnp.dot(
        columns,
        lax.all_gather(secondary, "inner", axis=0, tiled=True),
        preferred_element_type=jnp.float32,
    ).astype(jnp.bfloat16)
    reordered = (
        tokens.reshape(tok_rows, n_inner, n_outer, -1)
        .transpose(0, 2, 1, 3)
        .reshape(tok_rows, width)
    )
    columns = reordered
    gradient = lax.psum_scatter(
        rounded_term(columns, cotangent), ("outer", "inner"), scatter_dimension=0, tiled=True
    )
    total = lax.psum(jnp.sum(gradient * gradient), ("outer", "inner"))
    limit = 0.25 * math.sqrt(width * secondary.shape[1])
    factor = limit / jnp.maximum(jnp.sqrt(total), limit)
    master_new, m_code_new, v_code_new, m_scale_new, v_scale_new = adam_update(
        gradient, factor, master, m_code, v_code, m_scale, v_scale
    )
    secondary_new = lax.all_gather(master_new.astype(jnp.bfloat16), "outer", axis=0, tiled=True)
    return (projected, master_new, m_code_new, v_code_new, m_scale_new, v_scale_new, secondary_new)


def step_kernel(
    limit,
    tok_in, cot_in, sec_in, master_in, m_code_in, v_code_in, m_scale_in, v_scale_in,
    projected, master_new, m_code_new, v_code_new, m_scale_new, v_scale_new, sec_new,
    tok, cot, sec, master, m_code, v_code, m_scale, v_scale,
    send_a, recv_a, send_1, recv_1, send_2, recv_2, sum_3, send_3, recv_3,
    weights, sq_1, sq_2, sq_send, moments, seconds,
    sem_in, sem_a, sem_1, sem_2, sem_3, sem_w, sem_f, sem_q1, sem_q2, sem_g, sem_h, sem_p, sem_r,
):
    f32, bf16 = jnp.float32, jnp.bfloat16
    o, i = lax.axis_index("outer"), lax.axis_index("inner")
    n_z = 4
    core, z = o % 2, o // 2
    x, y = i % 2, i // 2
    to_x, to_y = i + 1 - 2 * x, i + 2 - 4 * y
    first = to_x * (1 - core) + to_y * core
    second = to_x * core + to_y * (1 - core)
    across = 3 - i
    mate = o + 1 - 2 * core
    rows = master.shape[0]
    half = sec.shape[0] // 2
    span = sec.shape[0]

    barrier = pltpu.get_barrier_semaphore()
    near = [(o, first), (o, second), (o, across)]
    far = [((o + d) % 8, i) for d in range(1, 8)]
    for peer in near + far:
        pl.semaphore_signal(barrier, inc=1, device_id=peer, device_id_type=MESH)

    loads = []

    def load(src, dst):
        loads.append(pltpu.make_async_copy(src, dst, sem_in.at[len(loads)]))
        loads[-1].start()

    load(cot_in, cot)
    groups = (across, second, first, i)
    pair = 2 * rows

    def columns_of(g, s):
        start = groups[g] * span + ((z + STEPS[s]) % n_z) * pair
        return pl.multiple_of(start, 128)

    for s in range(4):
        for g in range(4):
            columns = pl.ds(columns_of(g, s), pair)
            load(tok_in.at[:, columns], tok.at[:, columns])
        if s == 0:
            load(sec_in, sec)
    load(master_in, master)
    load(m_code_in, m_code)
    load(v_code_in, v_code)
    load(m_scale_in, m_scale)
    load(v_scale_in, v_scale)

    started = []

    def send(src, dst, sems, index, peer):
        copy = pltpu.make_async_remote_copy(
            src_ref=src, dst_ref=dst,
            send_sem=sems.at[0, index], recv_sem=sems.at[1, index],
            device_id=peer, device_id_type=MESH,
        )
        copy.start()
        started.append(copy)
        return copy

    def arrived(dst, sems, index):
        pltpu.make_async_remote_copy(
            src_ref=dst, dst_ref=dst,
            send_sem=sems.at[0, index], recv_sem=sems.at[1, index],
            device_id=(mate, i), device_id_type=MESH,
        ).wait_recv()

    def weight_part(j, part):
        third = half // 3
        return weights.at[j, core, pl.ds(part * third, third + part * third)]

    def send_weights(part):
        third = half // 3
        start = pl.multiple_of(core * half + part * third, 128)
        source = sec.at[pl.ds(start, third + part * third)]
        for index, peer in enumerate((first, second)):
            send(source, weight_part(i, part), sem_w, 2 * part + index, (o, peer))

    def partials(s, c):
        for g in range(4):
            start = pl.multiple_of(columns_of(g, s) + c * rows, 128)
            part = lax.dot_general(
                tok[:, pl.ds(start, rows)], cot[...], (((0,), (0,)), ((), ())),
                preferred_element_type=f32,
            )
            send_a[s, c, g] = part.astype(bf16)

    def for_both(s):
        for g in range(4):
            loads[1 + 4 * s + g + (s > 0)].wait()
        partials(s, 1 - core)
        if s == 0:
            pl.semaphore_wait(barrier, 10)
        send(send_a.at[s, 1 - core], recv_a.at[s], sem_a, s, (mate, i))
        partials(s, core)

    def chip_sum(q, s):
        own = send_a[s, core, (0, 2, 1, 3)[q]]
        return own.astype(f32) + recv_a[s, q].astype(f32)

    def to_first(s):
        arrived(recv_a.at[s], sem_a, s)
        for q in range(2):
            send_1[q, s] = chip_sum(q, s).astype(bf16)
            send(send_1.at[q, s], recv_1.at[q, s], sem_1, q * 4 + s, (o, first))

    def to_second(s):
        arrived(recv_1.at[0, s], sem_1, s)
        send_2[s] = (chip_sum(2, s) + recv_1[0, s].astype(f32)).astype(bf16)
        send(send_2.at[s], recv_2.at[s], sem_2, s, (o, second))

    def along_z(s):
        arrived(recv_1.at[1, s], sem_1, 4 + s)
        arrived(recv_2.at[s], sem_2, s)
        total = chip_sum(3, s) + recv_1[1, s].astype(f32) + recv_2[s].astype(f32)
        if STEPS[s]:
            d = STEPS[s]
            send_3[d - 1] = total.astype(bf16)
            peer = ((z + d) % n_z) * 2 + core
            send(send_3.at[d - 1], recv_3.at[d - 1], sem_3, d - 1, (peer, i))
        else:
            sum_3[...] = total

    loads[0].wait()
    for_both(0)
    for_both(1)
    to_first(0)
    for_both(2)
    to_first(1)
    for_both(3)
    to_second(0)
    to_first(2)
    to_second(1)
    to_first(3)
    along_z(0)
    to_second(2)
    along_z(1)
    to_second(3)
    along_z(2)
    along_z(3)

    loads[5].wait()
    send_weights(0)
    send_weights(1)
    arrived(weight_part(first, 0), sem_w, 0)
    send(weight_part(first, 0), weight_part(first, 0), sem_w, 4, (o, second))
    arrived(weight_part(second, 0), sem_w, 1)

    own_columns = tok[:, pl.ds(pl.multiple_of(i * span, 128), span)]
    out = jnp.dot(own_columns, sec[...], preferred_element_type=f32)

    for d in (1, 3, 2):
        arrived(recv_3.at[d - 1], sem_3, d - 1)
    gradient = sum_3[...]
    for d in range(1, 4):
        gradient = gradient + recv_3[d - 1].astype(f32)
    sum_3[...] = gradient

    squares = jnp.sum((gradient * gradient).reshape(rows // 8, 8, 128), axis=0)
    sq_send[0] = squares
    for d in range(1, 8):
        send(sq_send.at[0], sq_2.at[d - 1], sem_q2, d - 1, ((o + d) % 8, i))
    for copy in loads[18:]:
        copy.wait()
    height = rows // m_scale.shape[1]

    def block_mask(p):
        shape = (PIECE, m_scale.shape[1])
        row = lax.broadcasted_iota(jnp.int32, shape, 0) + p * PIECE
        return row // height == lax.broadcasted_iota(jnp.int32, shape, 1)

    def expand(p, scales):
        return jnp.sum(jnp.where(block_mask(p), scales, 0.0), axis=1, keepdims=True)

    pieces = rows // PIECE
    for p in range(pieces):
        part = pl.ds(p * PIECE, PIECE)
        moments[part, :] = 0.9 * (m_code[part, :].astype(f32) * expand(p, m_scale[...]))
        seconds[part, :] = 0.95 * (v_code[part, :].astype(f32) * expand(p, v_scale[...]))

    for d in range(1, 8):
        arrived(sq_2.at[d - 1], sem_q2, d - 1)
        squares = squares + sq_2[d - 1]
    sq_send[1] = squares
    for index, peer in enumerate((first, second, across)):
        send(sq_send.at[1], sq_1.at[index], sem_q1, index, (o, peer))
    arrived(weight_part(first, 1), sem_w, 2)
    send(weight_part(first, 1), weight_part(first, 1), sem_w, 5, (o, second))
    send(weights.at[first, core], weights.at[first, core], sem_f, 0, (mate, i))
    arrived(weight_part(second, 1), sem_w, 3)
    send(weights.at[second, core], weights.at[second, core], sem_f, 1, (mate, i))

    for index in range(3):
        arrived(sq_1.at[index], sem_q1, index)
        squares = squares + sq_1[index]
    square_sum = jnp.sum(jnp.sum(squares, axis=0, keepdims=True), axis=1, keepdims=True)
    factor = limit / jnp.maximum(jnp.sqrt(square_sum), limit)

    def new_rows(owner):
        return sec_new.at[pl.ds(pl.multiple_of(owner * rows, 128), rows)]

    def new_piece(owner, p):
        return sec_new.at[pl.ds(pl.multiple_of(owner * rows + p * PIECE, 128), PIECE)]

    for p in range(pieces):
        part = pl.ds(p * PIECE, PIECE)
        scaled = factor * sum_3[part, :]
        moment = moments[part, :] + 0.1 * scaled
        second_new = seconds[part, :] + 0.05 * scaled * scaled
        old = master[part, :]
        new = old - 0.01 * (moment / (jnp.sqrt(second_new) + 1e-08) + 0.1 * old)
        moments[part, :] = moment
        seconds[part, :] = second_new
        master_new[part, :] = new
        sec_new[pl.ds(pl.multiple_of(o * rows + p * PIECE, 128), PIECE), :] = new.astype(bf16)
        send(new_piece(o, p), new_piece(o, p), sem_p, p, (((z + 2) % n_z) * 2 + core, i))

    def neighbour(d):
        peer = (((z + d) % n_z) * 2 + core, i)
        return pltpu.make_async_remote_copy(
            src_ref=new_rows(o), dst_ref=new_rows(o),
            send_sem=sem_g.at[0, d - 1], recv_sem=sem_g.at[1, d - 1],
            device_id=peer, device_id_type=MESH,
        )

    guarded = [(z < n_z - 1, neighbour(1)), (z > 0, neighbour(3))]
    for needed, copy in guarded:
        pl.when(needed)(copy.start)
    send(new_rows(o), new_rows(o), sem_h, 0, (mate, i))

    m_row = jnp.zeros(m_scale.shape, f32)
    v_row = jnp.zeros(v_scale.shape, f32)
    for p in range(pieces):
        part = pl.ds(p * PIECE, PIECE)
        mask = block_mask(p)
        for values, codes, is_m in ((moments, m_code_new, True), (seconds, v_code_new, False)):
            value = values[part, :]
            tops = jnp.max(jnp.abs(value), axis=1, keepdims=True)
            top = jnp.max(jnp.where(mask, tops, 0.0), axis=0, keepdims=True)
            scale = top + 1e-06
            codes[part, :] = (value / expand(p, scale)).astype(bf16)
            if is_m:
                m_row = jnp.maximum(m_row, top)
            else:
                v_row = jnp.maximum(v_row, top)
    m_scale_new[...] = m_row + 1e-06
    v_scale_new[...] = v_row + 1e-06

    def product(j, h):
        start = pl.multiple_of(j * span + h * half, 128)
        return jnp.dot(tok[:, pl.ds(start, half)], weights[j, h], preferred_element_type=f32)

    def gathered(d):
        owner = ((z + n_z - d) % n_z) * 2 + core
        if d != 2:
            arrived(new_rows(owner), sem_g, d - 1)
        else:
            for p in range(pieces):
                arrived(new_piece(owner, p), sem_p, p)
            inside = (z > 0) & (z < n_z - 1)
            index = (2 * z + 2) % n_z
            end = (z // 2) * (n_z - 1)
            copy = pltpu.make_async_remote_copy(
                src_ref=new_rows(owner), dst_ref=new_rows(owner),
                send_sem=sem_r.at[0], recv_sem=sem_g.at[1, index],
                device_id=(end * 2 + core, i), device_id_type=MESH,
            )
            pl.when(inside)(copy.start)
            guarded.append((inside, copy))
        send(new_rows(owner), new_rows(owner), sem_h, d, (mate, i))

    out = out + product(first, core)
    out = out + product(second, core)
    gathered(2)
    arrived(weight_part(across, 0), sem_w, 4)
    arrived(weight_part(across, 1), sem_w, 5)
    send(weights.at[across, core], weights.at[across, core], sem_f, 2, (mate, i))
    out = out + product(across, core)
    for index, j in enumerate((second, first)):
        arrived(weights.at[j, 1 - core], sem_f, index)
        out = out + product(j, 1 - core)
    gathered(1)
    gathered(3)
    arrived(weights.at[across, 1 - core], sem_f, 2)
    out = out + product(across, 1 - core)
    projected[...] = out.astype(bf16)
    for d in range(4):
        owner = ((z + n_z - d) % n_z) * 2 + 1 - core
        arrived(new_rows(owner), sem_h, d)
    for copy in started:
        copy.wait_send()
    for needed, copy in guarded:
        pl.when(needed)(copy.wait_send)


def write_kernel(*refs):
    count = len(refs) // 2
    sems = refs[-1]
    copies = [
        pltpu.make_async_copy(refs[k], refs[count + k], sems.at[k]) for k in range(count)
    ]
    for copy in copies:
        copy.start()
    for copy in copies:
        copy.wait()


def fused_body(tokens, cotangent, secondary, master, m_code, v_code, m_scale, v_scale):
    f32, bf16 = jnp.float32, jnp.bfloat16
    rows, head = master.shape
    blocks = m_scale.shape[0]
    chunk = (rows, head)
    limit = 0.25 * math.sqrt(tokens.shape[1] * secondary.shape[1])
    vmem, dma = pltpu.VMEM, pltpu.SemaphoreType.DMA
    shapes = (
        ((tokens.shape[0], head), bf16),
        (chunk, f32),
        (chunk, bf16),
        (chunk, bf16),
        ((1, blocks), f32),
        ((1, blocks), f32),
        (secondary.shape, bf16),
    )
    work = 4 * tokens.shape[0] * tokens.shape[1] * head
    outs = pl.pallas_call(
        functools.partial(step_kernel, limit),
        out_shape=[vmem(shape, dtype) for shape, dtype in shapes],
        in_specs=[pl.BlockSpec(memory_space=pltpu.HBM)] * 8,
        out_specs=[pl.BlockSpec(memory_space=vmem)] * 7,
        scratch_shapes=[
            vmem(tokens.shape, bf16),
            vmem(cotangent.shape, bf16),
            vmem(secondary.shape, bf16),
            vmem(chunk, f32),
            vmem(chunk, bf16),
            vmem(chunk, bf16),
            vmem((1, blocks), f32),
            vmem((1, blocks), f32),
            vmem((4, 2, 4) + chunk, bf16),
            vmem((4, 4) + chunk, bf16),
            vmem((2, 4) + chunk, bf16),
            vmem((2, 4) + chunk, bf16),
            vmem((4,) + chunk, bf16),
            vmem((4,) + chunk, bf16),
            vmem(chunk, f32),
            vmem((3,) + chunk, bf16),
            vmem((3,) + chunk, bf16),
            vmem((4, 2, secondary.shape[0] // 2, head), bf16),
            vmem((3, 8, head), f32),
            vmem((7, 8, head), f32),
            vmem((2, 8, head), f32),
            vmem(chunk, f32),
            vmem(chunk, f32),
            dma((23,)),
            dma((2, 4)),
            dma((2, 8)),
            dma((2, 4)),
            dma((2, 3)),
            dma((2, 6)),
            dma((2, 3)),
            dma((2, 3)),
            dma((2, 7)),
            dma((2, 3)),
            dma((2, 4)),
            dma((2, 3)),
            dma((1,)),
        ],
        compiler_params=pltpu.CompilerParams(
            collective_id=0, has_side_effects=True, vmem_limit_bytes=VMEM_BYTES
        ),
        cost_estimate=pl.CostEstimate(flops=work, bytes_accessed=8 << 20, transcendentals=0),
    )(
        tokens, cotangent, secondary, master, m_code, v_code,
        m_scale.reshape(1, blocks), v_scale.reshape(1, blocks),
    )
    outs = pl.pallas_call(
        write_kernel,
        out_shape=[jax.ShapeDtypeStruct(shape, dtype) for shape, dtype in shapes],
        in_specs=[pl.BlockSpec(memory_space=vmem)] * 7,
        out_specs=[pl.BlockSpec(memory_space=pltpu.HBM)] * 7,
        scratch_shapes=[dma((7,))],
        compiler_params=pltpu.CompilerParams(vmem_limit_bytes=4 << 20),
    )(*outs)
    return (*outs[:4], outs[4].reshape(blocks), outs[5].reshape(blocks), outs[6])


def fits(mesh):
    return mesh.shape["outer"] == 8 and mesh.shape["inner"] == 4


def solution(mesh):
    in_specs = (
        P(("outer", "inner"), None),
        P(("outer", "inner"), None),
        P("inner", None),
        P(("inner", "outer"), None),
        P(("inner", "outer"), None),
        P(("inner", "outer"), None),
        P(("inner", "outer")),
        P(("inner", "outer")),
    )
    out_specs = (
        P(("outer", "inner"), None),
        P(("inner", "outer"), None),
        P(("inner", "outer"), None),
        P(("inner", "outer"), None),
        P(("inner", "outer")),
        P(("inner", "outer")),
        P("inner", None),
    )
    program = fused_body if fits(mesh) else body
    return jax.shard_map(
        program, mesh=mesh, in_specs=in_specs, out_specs=out_specs, check_vma=False
    )
```

```python
import functools
import math

import jax
import jax.numpy as jnp
from jax import lax
from jax.experimental import pallas as pl
from jax.experimental.pallas import tpu as pltpu
from jax.sharding import PartitionSpec as P

MESH = pl.DeviceIdType.MESH
PIECE = 128
VMEM_BYTES = 60 * 1024 * 1024
STEPS = (2, 1, 3, 0)


def adam_update(gradient, factor, master, m_code, v_code, m_scale, v_scale):
    blocks = m_scale.shape[0]
    height = master.shape[0] // blocks
    shaped = (blocks, height, master.shape[1])
    m_old = (m_code.astype(jnp.float32).reshape(shaped) * m_scale[:, None, None]).reshape(
        master.shape
    )
    v_old = (v_code.astype(jnp.float32).reshape(shaped) * v_scale[:, None, None]).reshape(
        master.shape
    )
    scaled = factor * gradient
    moment = 0.9 * m_old + 0.1 * scaled
    second = 0.95 * v_old + 0.05 * scaled * scaled
    master_new = master - 0.01 * (moment / (jnp.sqrt(second) + 1e-08) + 0.1 * master)
    moment_blocks = moment.reshape(blocks, -1)
    second_blocks = second.reshape(blocks, -1)
    m_scale_new = jnp.max(jnp.abs(moment_blocks), axis=1) + 1e-06
    v_scale_new = jnp.max(second_blocks, axis=1) + 1e-06
    m_code_new = (moment_blocks / m_scale_new[:, None]).reshape(master.shape).astype(jnp.bfloat16)
    v_code_new = (second_blocks / v_scale_new[:, None]).reshape(master.shape).astype(jnp.bfloat16)
    return (master_new, m_code_new, v_code_new, m_scale_new, v_scale_new)


def rounded_term(columns, cotangent):
    part = lax.dot_general(
        columns, cotangent, (((0,), (0,)), ((), ())), preferred_element_type=jnp.float32
    )
    part = lax.optimization_barrier(part.astype(jnp.bfloat16))
    return part.astype(jnp.float32)


def body(tokens, cotangent, secondary, master, m_code, v_code, m_scale, v_scale):
    tok_rows = tokens.shape[0]
    width = tokens.shape[1]
    n_outer = lax.axis_size("outer")
    n_inner = lax.axis_size("inner")
    columns = tokens
    projected = jnp.dot(
        columns,
        lax.all_gather(secondary, "inner", axis=0, tiled=True),
        preferred_element_type=jnp.float32,
    ).astype(jnp.bfloat16)
    reordered = (
        tokens.reshape(tok_rows, n_inner, n_outer, -1)
        .transpose(0, 2, 1, 3)
        .reshape(tok_rows, width)
    )
    columns = reordered
    gradient = lax.psum_scatter(
        rounded_term(columns, cotangent), ("outer", "inner"), scatter_dimension=0, tiled=True
    )
    total = lax.psum(jnp.sum(gradient * gradient), ("outer", "inner"))
    limit = 0.25 * math.sqrt(width * secondary.shape[1])
    factor = limit / jnp.maximum(jnp.sqrt(total), limit)
    master_new, m_code_new, v_code_new, m_scale_new, v_scale_new = adam_update(
        gradient, factor, master, m_code, v_code, m_scale, v_scale
    )
    secondary_new = lax.all_gather(master_new.astype(jnp.bfloat16), "outer", axis=0, tiled=True)
    return (projected, master_new, m_code_new, v_code_new, m_scale_new, v_scale_new, secondary_new)


def step_kernel(
    limit,
    tok_in, cot_in, sec_in, master_in, m_code_in, v_code_in, m_scale_in, v_scale_in,
    projected, master_new, m_code_new, v_code_new, m_scale_new, v_scale_new, sec_new,
    tok, cot, sec, master, m_code, v_code, m_scale, v_scale,
    send_a, recv_a, send_1, recv_1, send_2, recv_2, sum_3, send_3, recv_3,
    weights, sq_1, sq_2, sq_send, moments, seconds,
    sem_in, sem_a, sem_1, sem_2, sem_3, sem_w, sem_f, sem_q1, sem_q2, sem_g, sem_h, sem_p, sem_r,
):
    f32, bf16 = jnp.float32, jnp.bfloat16
    o, i = lax.axis_index("outer"), lax.axis_index("inner")
    n_z = 4
    core, z = o % 2, o // 2
    x, y = i % 2, i // 2
    to_x, to_y = i + 1 - 2 * x, i + 2 - 4 * y
    first = to_x * (1 - core) + to_y * core
    second = to_x * core + to_y * (1 - core)
    across = 3 - i
    mate = o + 1 - 2 * core
    rows = master.shape[0]
    half = sec.shape[0] // 2
    span = sec.shape[0]

    barrier = pltpu.get_barrier_semaphore()
    near = [(o, first), (o, second), (o, across)]
    far = [((o + d) % 8, i) for d in range(1, 8)]
    for peer in near + far:
        pl.semaphore_signal(barrier, inc=1, device_id=peer, device_id_type=MESH)

    loads = []

    def load(src, dst):
        loads.append(pltpu.make_async_copy(src, dst, sem_in.at[len(loads)]))
        loads[-1].start()

    load(cot_in, cot)
    groups = (across, second, first, i)
    pair = 2 * rows

    def columns_of(g, s):
        start = groups[g] * span + ((z + STEPS[s]) % n_z) * pair
        return pl.multiple_of(start, 128)

    for s in range(4):
        for g in range(4):
            columns = pl.ds(columns_of(g, s), pair)
            load(tok_in.at[:, columns], tok.at[:, columns])
        if s == 0:
            load(sec_in, sec)
    load(master_in, master)
    load(m_code_in, m_code)
    load(v_code_in, v_code)
    load(m_scale_in, m_scale)
    load(v_scale_in, v_scale)

    started = []

    def send(src, dst, sems, index, peer):
        copy = pltpu.make_async_remote_copy(
            src_ref=src, dst_ref=dst,
            send_sem=sems.at[0, index], recv_sem=sems.at[1, index],
            device_id=peer, device_id_type=MESH,
        )
        copy.start()
        started.append(copy)
        return copy

    def arrived(dst, sems, index):
        pltpu.make_async_remote_copy(
            src_ref=dst, dst_ref=dst,
            send_sem=sems.at[0, index], recv_sem=sems.at[1, index],
            device_id=(mate, i), device_id_type=MESH,
        ).wait_recv()

    def weight_part(j, part):
        third = half // 3
        return weights.at[j, core, pl.ds(2 * part * third, (2 - part) * third)]

    def send_weights(part):
        third = half // 3
        start = pl.multiple_of(core * half + 2 * part * third, 128)
        source = sec.at[pl.ds(start, (2 - part) * third)]
        for index, peer in enumerate((first, second)):
            send(source, weight_part(i, part), sem_w, 2 * part + index, (o, peer))

    def partials(s, c):
        for g in range(4):
            start = pl.multiple_of(columns_of(g, s) + c * rows, 128)
            part = lax.dot_general(
                tok[:, pl.ds(start, rows)], cot[...], (((0,), (0,)), ((), ())),
                preferred_element_type=f32,
            )
            send_a[s, c, g] = part.astype(bf16)

    def for_both(s):
        for g in range(4):
            loads[1 + 4 * s + g + (s > 0)].wait()
        partials(s, 1 - core)
        if s == 0:
            pl.semaphore_wait(barrier, 10)
        send(send_a.at[s, 1 - core], recv_a.at[s], sem_a, s, (mate, i))
        partials(s, core)

    def chip_sum(q, s):
        own = send_a[s, core, (0, 2, 1, 3)[q]]
        return own.astype(f32) + recv_a[s, q].astype(f32)

    def to_first(s):
        arrived(recv_a.at[s], sem_a, s)
        for q in range(2):
            send_1[q, s] = chip_sum(q, s).astype(bf16)
            send(send_1.at[q, s], recv_1.at[q, s], sem_1, q * 4 + s, (o, first))

    def to_second(s):
        arrived(recv_1.at[0, s], sem_1, s)
        send_2[s] = (chip_sum(2, s) + recv_1[0, s].astype(f32)).astype(bf16)
        send(send_2.at[s], recv_2.at[s], sem_2, s, (o, second))

    def along_z(s):
        arrived(recv_1.at[1, s], sem_1, 4 + s)
        arrived(recv_2.at[s], sem_2, s)
        total = chip_sum(3, s) + recv_1[1, s].astype(f32) + recv_2[s].astype(f32)
        if STEPS[s]:
            d = STEPS[s]
            send_3[d - 1] = total.astype(bf16)
            peer = ((z + d) % n_z) * 2 + core
            send(send_3.at[d - 1], recv_3.at[d - 1], sem_3, d - 1, (peer, i))
        else:
            sum_3[...] = total

    loads[0].wait()
    for_both(0)
    loads[5].wait()
    send_weights(0)
    for_both(1)
    to_first(0)
    for_both(2)
    to_first(1)
    for_both(3)
    to_second(0)
    to_first(2)
    to_second(1)
    to_first(3)
    along_z(0)
    to_second(2)
    along_z(1)
    to_second(3)
    along_z(2)
    along_z(3)

    send_weights(1)
    arrived(weight_part(first, 0), sem_w, 0)
    send(weight_part(first, 0), weight_part(first, 0), sem_w, 4, (o, second))
    arrived(weight_part(second, 0), sem_w, 1)

    own_columns = tok[:, pl.ds(pl.multiple_of(i * span, 128), span)]
    out = jnp.dot(own_columns, sec[...], preferred_element_type=f32)

    for d in (1, 3, 2):
        arrived(recv_3.at[d - 1], sem_3, d - 1)
    gradient = sum_3[...]
    for d in range(1, 4):
        gradient = gradient + recv_3[d - 1].astype(f32)
    sum_3[...] = gradient

    squares = jnp.sum((gradient * gradient).reshape(rows // 8, 8, 128), axis=0)
    sq_send[0] = squares
    for d in range(1, 8):
        send(sq_send.at[0], sq_2.at[d - 1], sem_q2, d - 1, ((o + d) % 8, i))
    for copy in loads[18:]:
        copy.wait()
    height = rows // m_scale.shape[1]

    def block_mask(p):
        shape = (PIECE, m_scale.shape[1])
        row = lax.broadcasted_iota(jnp.int32, shape, 0) + p * PIECE
        return row // height == lax.broadcasted_iota(jnp.int32, shape, 1)

    def expand(p, scales):
        return jnp.sum(jnp.where(block_mask(p), scales, 0.0), axis=1, keepdims=True)

    pieces = rows // PIECE
    for p in range(pieces):
        part = pl.ds(p * PIECE, PIECE)
        moments[part, :] = 0.9 * (m_code[part, :].astype(f32) * expand(p, m_scale[...]))
        seconds[part, :] = 0.95 * (v_code[part, :].astype(f32) * expand(p, v_scale[...]))

    for d in range(1, 8):
        arrived(sq_2.at[d - 1], sem_q2, d - 1)
        squares = squares + sq_2[d - 1]
    sq_send[1] = squares
    for index, peer in enumerate((first, second, across)):
        send(sq_send.at[1], sq_1.at[index], sem_q1, index, (o, peer))
    arrived(weight_part(first, 1), sem_w, 2)
    send(weight_part(first, 1), weight_part(first, 1), sem_w, 5, (o, second))
    send(weights.at[first, core], weights.at[first, core], sem_f, 0, (mate, i))
    arrived(weight_part(second, 1), sem_w, 3)
    send(weights.at[second, core], weights.at[second, core], sem_f, 1, (mate, i))

    for index in range(3):
        arrived(sq_1.at[index], sem_q1, index)
        squares = squares + sq_1[index]
    square_sum = jnp.sum(jnp.sum(squares, axis=0, keepdims=True), axis=1, keepdims=True)
    factor = limit / jnp.maximum(jnp.sqrt(square_sum), limit)

    def new_rows(owner):
        return sec_new.at[pl.ds(pl.multiple_of(owner * rows, 128), rows)]

    def new_piece(owner, p):
        return sec_new.at[pl.ds(pl.multiple_of(owner * rows + p * PIECE, 128), PIECE)]

    for p in range(pieces):
        part = pl.ds(p * PIECE, PIECE)
        scaled = factor * sum_3[part, :]
        moment = moments[part, :] + 0.1 * scaled
        second_new = seconds[part, :] + 0.05 * scaled * scaled
        old = master[part, :]
        new = old - 0.01 * (moment / (jnp.sqrt(second_new) + 1e-08) + 0.1 * old)
        moments[part, :] = moment
        seconds[part, :] = second_new
        master_new[part, :] = new
        sec_new[pl.ds(pl.multiple_of(o * rows + p * PIECE, 128), PIECE), :] = new.astype(bf16)
        send(new_piece(o, p), new_piece(o, p), sem_p, p, (((z + 2) % n_z) * 2 + core, i))

    def neighbour(d):
        peer = (((z + d) % n_z) * 2 + core, i)
        return pltpu.make_async_remote_copy(
            src_ref=new_rows(o), dst_ref=new_rows(o),
            send_sem=sem_g.at[0, d - 1], recv_sem=sem_g.at[1, d - 1],
            device_id=peer, device_id_type=MESH,
        )

    guarded = [(z < n_z - 1, neighbour(1)), (z > 0, neighbour(3))]
    for needed, copy in guarded:
        pl.when(needed)(copy.start)
    send(new_rows(o), new_rows(o), sem_h, 0, (mate, i))

    m_row = jnp.zeros(m_scale.shape, f32)
    v_row = jnp.zeros(v_scale.shape, f32)
    for p in range(pieces):
        part = pl.ds(p * PIECE, PIECE)
        mask = block_mask(p)
        for values, codes, is_m in ((moments, m_code_new, True), (seconds, v_code_new, False)):
            value = values[part, :]
            tops = jnp.max(jnp.abs(value), axis=1, keepdims=True)
            top = jnp.max(jnp.where(mask, tops, 0.0), axis=0, keepdims=True)
            scale = top + 1e-06
            codes[part, :] = (value / expand(p, scale)).astype(bf16)
            if is_m:
                m_row = jnp.maximum(m_row, top)
            else:
                v_row = jnp.maximum(v_row, top)
    m_scale_new[...] = m_row + 1e-06
    v_scale_new[...] = v_row + 1e-06

    def product(j, h):
        start = pl.multiple_of(j * span + h * half, 128)
        return jnp.dot(tok[:, pl.ds(start, half)], weights[j, h], preferred_element_type=f32)

    def gathered(d):
        owner = ((z + n_z - d) % n_z) * 2 + core
        if d != 2:
            arrived(new_rows(owner), sem_g, d - 1)
        else:
            for p in range(pieces):
                arrived(new_piece(owner, p), sem_p, p)
            inside = (z > 0) & (z < n_z - 1)
            index = (2 * z + 2) % n_z
            end = (z // 2) * (n_z - 1)
            copy = pltpu.make_async_remote_copy(
                src_ref=new_rows(owner), dst_ref=new_rows(owner),
                send_sem=sem_r.at[0], recv_sem=sem_g.at[1, index],
                device_id=(end * 2 + core, i), device_id_type=MESH,
            )
            pl.when(inside)(copy.start)
            guarded.append((inside, copy))
        send(new_rows(owner), new_rows(owner), sem_h, d, (mate, i))

    out = out + product(first, core)
    out = out + product(second, core)
    gathered(2)
    arrived(weight_part(across, 0), sem_w, 4)
    arrived(weight_part(across, 1), sem_w, 5)
    send(weights.at[across, core], weights.at[across, core], sem_f, 2, (mate, i))
    out = out + product(across, core)
    for index, j in enumerate((second, first)):
        arrived(weights.at[j, 1 - core], sem_f, index)
        out = out + product(j, 1 - core)
    gathered(1)
    gathered(3)
    arrived(weights.at[across, 1 - core], sem_f, 2)
    out = out + product(across, 1 - core)
    projected[...] = out.astype(bf16)
    for d in range(4):
        owner = ((z + n_z - d) % n_z) * 2 + 1 - core
        arrived(new_rows(owner), sem_h, d)
    for copy in started:
        copy.wait_send()
    for needed, copy in guarded:
        pl.when(needed)(copy.wait_send)


def write_kernel(*refs):
    count = len(refs) // 2
    sems = refs[-1]
    copies = [
        pltpu.make_async_copy(refs[k], refs[count + k], sems.at[k]) for k in range(count)
    ]
    for copy in copies:
        copy.start()
    for copy in copies:
        copy.wait()


def fused_body(tokens, cotangent, secondary, master, m_code, v_code, m_scale, v_scale):
    f32, bf16 = jnp.float32, jnp.bfloat16
    rows, head = master.shape
    blocks = m_scale.shape[0]
    chunk = (rows, head)
    limit = 0.25 * math.sqrt(tokens.shape[1] * secondary.shape[1])
    vmem, dma = pltpu.VMEM, pltpu.SemaphoreType.DMA
    shapes = (
        ((tokens.shape[0], head), bf16),
        (chunk, f32),
        (chunk, bf16),
        (chunk, bf16),
        ((1, blocks), f32),
        ((1, blocks), f32),
        (secondary.shape, bf16),
    )
    work = 4 * tokens.shape[0] * tokens.shape[1] * head
    outs = pl.pallas_call(
        functools.partial(step_kernel, limit),
        out_shape=[vmem(shape, dtype) for shape, dtype in shapes],
        in_specs=[pl.BlockSpec(memory_space=pltpu.HBM)] * 8,
        out_specs=[pl.BlockSpec(memory_space=vmem)] * 7,
        scratch_shapes=[
            vmem(tokens.shape, bf16),
            vmem(cotangent.shape, bf16),
            vmem(secondary.shape, bf16),
            vmem(chunk, f32),
            vmem(chunk, bf16),
            vmem(chunk, bf16),
            vmem((1, blocks), f32),
            vmem((1, blocks), f32),
            vmem((4, 2, 4) + chunk, bf16),
            vmem((4, 4) + chunk, bf16),
            vmem((2, 4) + chunk, bf16),
            vmem((2, 4) + chunk, bf16),
            vmem((4,) + chunk, bf16),
            vmem((4,) + chunk, bf16),
            vmem(chunk, f32),
            vmem((3,) + chunk, bf16),
            vmem((3,) + chunk, bf16),
            vmem((4, 2, secondary.shape[0] // 2, head), bf16),
            vmem((3, 8, head), f32),
            vmem((7, 8, head), f32),
            vmem((2, 8, head), f32),
            vmem(chunk, f32),
            vmem(chunk, f32),
            dma((23,)),
            dma((2, 4)),
            dma((2, 8)),
            dma((2, 4)),
            dma((2, 3)),
            dma((2, 6)),
            dma((2, 3)),
            dma((2, 3)),
            dma((2, 7)),
            dma((2, 3)),
            dma((2, 4)),
            dma((2, 3)),
            dma((1,)),
        ],
        compiler_params=pltpu.CompilerParams(
            collective_id=0, has_side_effects=True, vmem_limit_bytes=VMEM_BYTES
        ),
        cost_estimate=pl.CostEstimate(flops=work, bytes_accessed=8 << 20, transcendentals=0),
    )(
        tokens, cotangent, secondary, master, m_code, v_code,
        m_scale.reshape(1, blocks), v_scale.reshape(1, blocks),
    )
    outs = pl.pallas_call(
        write_kernel,
        out_shape=[jax.ShapeDtypeStruct(shape, dtype) for shape, dtype in shapes],
        in_specs=[pl.BlockSpec(memory_space=vmem)] * 7,
        out_specs=[pl.BlockSpec(memory_space=pltpu.HBM)] * 7,
        scratch_shapes=[dma((7,))],
        compiler_params=pltpu.CompilerParams(vmem_limit_bytes=4 << 20),
    )(*outs)
    return (*outs[:4], outs[4].reshape(blocks), outs[5].reshape(blocks), outs[6])


def fits(mesh):
    return mesh.shape["outer"] == 8 and mesh.shape["inner"] == 4


def solution(mesh):
    in_specs = (
        P(("outer", "inner"), None),
        P(("outer", "inner"), None),
        P("inner", None),
        P(("inner", "outer"), None),
        P(("inner", "outer"), None),
        P(("inner", "outer"), None),
        P(("inner", "outer")),
        P(("inner", "outer")),
    )
    out_specs = (
        P(("outer", "inner"), None),
        P(("inner", "outer"), None),
        P(("inner", "outer"), None),
        P(("inner", "outer"), None),
        P(("inner", "outer")),
        P(("inner", "outer")),
        P("inner", None),
    )
    program = fused_body if fits(mesh) else body
    return jax.shard_map(
        program, mesh=mesh, in_specs=in_specs, out_specs=out_specs, check_vma=False
    )
```
